256 devices in a mesh: inline: 16 (over z, core), xline: 4 (over y), tm: 4 (over x).
Axes of the slice: x: 4, y: 4, z: 8, core: 2. Of those that a mesh axis runs over, the one named last changes fastest.
Arguments:
- observed: float32 [64, 256, 2048], P('inline', 'xline', 'tm'), may hold values from -18 to 18
- start_model: float32 [64, 256, 2048], P('inline', 'xline', 'tm'), may hold values from -6 to 6
- wavelet: float32 [64], replicated, may hold values from -0.375 to 0.375
Outputs:
- model_out: float32 [64, 256, 2048], P('inline', 'xline', 'tm')
- dual_out: float32 [3, 64, 256, 2048], P(None, 'inline', 'xline', 'tm')
- misfits: float32 [4], replicated
The draws below stay inside these ranges and needn't reach their ends.
All inputs are finite; a program needn't handle non-finite values.
Results may differ from the reference program's by a relative error of at most 0.0001.
Values sent between devices are 32-bit elements; how exact they have to be, the bound alone decides.
A program may use at most 64 MiB of HBM per device.

```python
import jax
import jax.numpy as jnp
from jax import lax

TAPS = 64
ITERS = 4
INLINES = 64
XLINES = 256
SAMPLES = 2048


def draw_observed(key, part):
    key = jax.random.fold_in(key, 7)
    key_base, key_rough = jax.random.split(key)
    shape_all = (INLINES, XLINES, SAMPLES)
    inline_ramp = 1.0 + 2.0 * jnp.arange(INLINES, dtype=jnp.float32)[:, None, None] / (INLINES - 1)
    roughness = jax.random.uniform(key_rough, shape_all, jnp.float32, 0.5, 1.5)
    baseline = jnp.clip(jax.random.normal(key_base, shape_all, jnp.float32), -4.0, 4.0)
    return baseline * roughness * inline_ramp


def level_of(key, extent, shards, smallest, high):
    loudness, own = 1.0, jax.random.fold_in(key, 6)
    for axis_at, blocks in shards:
        draws = jnp.exp(jax.random.uniform(jax.random.fold_in(own, axis_at), (blocks,), jnp.float32, smallest / len(shards), high / len(shards)))
        loudness = loudness * jnp.repeat(draws, extent[axis_at] // blocks).reshape([-1 if axis == axis_at else 1 for axis in range(len(extent))])
    return loudness


def normal_values(rng, shape, deviation, most, shards=(), kind=jnp.bfloat16):
    result = jax.random.normal(rng, shape, jnp.float32) * deviation
    if len(shards) > 0:
        result = level_of(rng, shape, shards, -0.22, 0.18) * result
    return jnp.clip(result, min=-most, max=most).astype(kind)


def setup_inputs(seed: int = 0) -> dict:
    arg_keys = jax.random.split(jax.random.key(seed), 4)
    return {
        "observed": draw_observed(jax.random.fold_in(arg_keys[3], 71), 0),
        "start_model": normal_values(arg_keys[1], (INLINES, XLINES, SAMPLES), 1.0, 6.0, ((0, 16), (1, 4), (2, 4)), jnp.float32),
        "wavelet": normal_values(arg_keys[2], (TAPS,), 256 ** -0.5, 0.375, (), jnp.float32),
    }


tau_step = 0.1
sigma_step = 0.5
tv_weight = 1.0

def forward_slab(slab, wavelet):
    rim_width = TAPS // 2 + 1
    padded = jnp.pad(slab, ((0, 0), (rim_width, rim_width)))
    reflect = padded[:, 1:] - padded[:, :-1]
    sample_total = slab.shape[1]
    synthetic = jnp.zeros(slab.shape, jnp.float32)
    for tap_index in range(TAPS):
        begin = 2 * rim_width - 1 - tap_index
        synthetic = synthetic + wavelet[tap_index] * reflect[:, begin:begin + sample_total]
    return synthetic

def adjoint_slab(slab, wavelet):
    rim_width = TAPS // 2 + 1
    padded = jnp.pad(slab, ((0, 0), (rim_width, rim_width)))
    slope = padded[:, :-1] - padded[:, 1:]
    sample_total = slab.shape[1]
    backproj = jnp.zeros(slab.shape, jnp.float32)
    for tap_index in range(TAPS):
        backproj = backproj + wavelet[tap_index] * slope[:, tap_index:tap_index + sample_total]
    return backproj

def slopes_of(field):
    padded = jnp.pad(field, ((0, 1), (0, 1), (0, 1)))
    return jnp.stack([padded[1:, :-1, :-1] - field, padded[:-1, 1:, :-1] - field, padded[:-1, :-1, 1:] - field])

def divergence_term(dual_field):
    padded = jnp.pad(dual_field, ((0, 0), (1, 0), (1, 0), (1, 0)))
    first = padded[0, :-1, 1:, 1:] - dual_field[0]
    second = padded[1, 1:, :-1, 1:] - dual_field[1]
    third = padded[2, 1:, 1:, :-1] - dual_field[2]
    return first + second + third

def reference(observed, start_model, wavelet):
    model_now = start_model
    extrapolated = start_model
    dual_field = jnp.zeros((3,) + start_model.shape, jnp.float32)
    cell_total = INLINES * XLINES * SAMPLES
    misfit_list = []
    for sweep_index in range(ITERS):
        trial = dual_field + sigma_step * slopes_of(extrapolated)
        magnitude = jnp.sqrt(lax.optimization_barrier(jnp.sum(trial * trial, axis=0)))
        dual_field = trial / jnp.maximum(1.0, magnitude / tv_weight)
        synthetic = lax.map(lambda slab: forward_slab(slab, wavelet), model_now)
        residual = synthetic - observed
        misfit_list.append(jnp.sum(residual * residual) / cell_total)
        backproj = lax.map(lambda slab: adjoint_slab(slab, wavelet), residual)
        updated = model_now - tau_step * (backproj + divergence_term(dual_field))
        extrapolated = 2.0 * updated - model_now
        model_now = updated
    return (model_now, dual_field, jnp.stack(misfit_list))
```

```python
import functools

import jax
import jax.numpy as jnp
from jax import lax
from jax.experimental import pallas as pl
from jax.experimental.pallas import tpu as pltpu
from jax.sharding import PartitionSpec as P

TAPS = 64
ITERS = 4
LANES = 128
TILE = 256
ROWS = 16
MESH = pl.DeviceIdType.MESH
F32 = jnp.float32
BF16 = jnp.bfloat16

tau_step = 0.1
sigma_step = 0.5
tv_weight = 1.0

TO_HI, TO_LO, TO_JLO, TO_JHI, TO_THI, TO_TLO, E_IMJP, E_IPJM, E_IMTP, E_IPTM, E_JMTP, E_JPTM = range(12)
MESSAGES = {
    TO_HI: (1, 0, 0),
    TO_LO: (-1, 0, 0),
    TO_JLO: (0, -1, 0),
    TO_JHI: (0, 1, 0),
    TO_THI: (0, 0, 1),
    TO_TLO: (0, 0, -1),
    E_IMJP: (1, -1, 0),
    E_IPJM: (-1, 1, 0),
    E_IMTP: (1, 0, -1),
    E_IPTM: (-1, 0, 1),
    E_JMTP: (0, 1, -1),
    E_JPTM: (0, -1, 1),
}


def split(x):
    hi = x.astype(BF16)
    lo = (x - hi.astype(F32)).astype(BF16)
    return hi, lo


def lane_ids(shape):
    return lax.broadcasted_iota(jnp.int32, shape, len(shape) - 1)


def circulant(row):
    sub = lax.broadcasted_iota(jnp.int32, (8, TILE), 0)
    first = row
    for s in range(1, 8):
        first = jnp.where(sub == s, pltpu.roll(row, s, 1), first)
    return jnp.concatenate([first] + [pltpu.roll(first, 8 * g, 1) for g in range(1, TILE // 8)], axis=0)


def dot32(a, b):
    return jnp.dot(a, b, preferred_element_type=F32, precision=lax.Precision.HIGHEST)


def kernel(
    obs_hbm, start_hbm, wav, mout, dout, misf,
    X, ms, obs, grad, am, mc, ril, rih, rjl, rjh, rtl, rth, rol, roh,
    eimjp, eipjm, eimtp, eiptm, ejmtp, ejptm,
    jlo, jhi, tlo, thi, olo, ohi, clo, chi,
    pd0, pd1, pd2, pm, pj, part, allsum, r1, r2,
    tG, tA0, tA1, tB,
    in_sem, send_sem, recv_sem, osend, orecv, s1s, s1r, s2s, s2r,
):
    n_i, n_j, n_t = lax.axis_size("inline"), lax.axis_size("xline"), lax.axis_size("tm")
    me_i, me_j, me_t = lax.axis_index("inline"), lax.axis_index("xline"), lax.axis_index("tm")

    def at(di, dj, dt):
        return (
            lax.rem(me_i + (di + n_i), n_i),
            lax.rem(me_j + (dj + n_j), n_j),
            lax.rem(me_t + (dt + n_t), n_t),
        )

    i_peers = [(d, 0, 0) for d in range(1, n_i)]
    p_peers = [(0, d // n_t, d % n_t) for d in range(1, n_j * n_t)]
    friends = {tuple(o % n for o, n in zip(off, (n_i, n_j, n_t))) for off in MESSAGES.values()}
    friends = sorted(friends | set(i_peers) | set(p_peers))

    barrier = pltpu.get_barrier_semaphore()
    for off in friends:
        pl.semaphore_signal(barrier, inc=1, device_id=at(*off), device_id_type=MESH)

    loads = []
    for b in range(4):
        cols = pl.ds(b * LANES, LANES)
        loads.append(pltpu.make_async_copy(start_hbm.at[:, :, cols], X.at[0, :, b, 0:64, :], in_sem.at[b]))
    for b in range(4):
        cols = pl.ds(b * LANES, LANES)
        loads.append(pltpu.make_async_copy(obs_hbm.at[:, :, cols], obs.at[:, b], in_sem.at[4 + b]))
    for load in loads:
        load.start()

    not_i0 = (me_i > 0).astype(F32)
    not_in = (me_i < n_i - 1).astype(F32)
    not_j0 = (me_j > 0).astype(F32)
    not_jn = (me_j < n_j - 1).astype(F32)
    not_t0 = (me_t > 0).astype(F32)
    not_tn = (me_t < n_t - 1).astype(F32)

    def build_tables():
        ids = lane_ids((8, TILE))
        w = jnp.zeros((8, TILE), F32)
        for k in range(TAPS):
            w = jnp.where(ids == k, wav[k], w)
        c = w - pltpu.roll(w, 1, 1)
        half = TAPS // 2 + 1
        circ_g = circulant(pltpu.roll(c, TILE - half, 1))
        rev = jnp.zeros((8, TILE), F32)
        for k in range(TAPS + 1):
            left = wav[k] if k < TAPS else 0.0
            right = wav[k - 1] if k > 0 else 0.0
            rev = jnp.where(ids == (half - k) % TILE, left - right, rev)
        circ_d = circulant(rev)
        r = lax.broadcasted_iota(jnp.int32, (TILE, TILE), 0)
        near = jnp.abs(r - lane_ids((TILE, TILE))) < LANES

        def store(table, rows, value):
            hi, lo = split(value)
            table[rows : rows + TILE, :] = hi
            table[2 * TILE + rows : 3 * TILE + rows, :] = hi
            table[4 * TILE + rows : 5 * TILE + rows, :] = lo

        g_far = jnp.where(near, 0.0, circ_g)
        d_far = jnp.where(near, 0.0, circ_d)
        store(tG, 0, jnp.where(near, circ_g, 0.0))
        store(tG, TILE, g_far)
        store(tB, 0, jnp.where(near, circ_d, 0.0))
        store(tB, TILE, d_far)
        circ_a = dot32(circ_g, circ_d)
        edge = dot32(g_far, d_far)
        a_near = jnp.where(near, circ_a, 0.0)
        a_far = jnp.where(near, 0.0, circ_a)
        store(tA0, 0, a_near - jnp.where(r < LANES, (1.0 - not_t0) * edge, 0.0))
        store(tA0, TILE, a_far)
        store(tA1, 0, a_near - jnp.where(r < LANES, 0.0, (1.0 - not_tn) * edge))
        store(tA1, TILE, a_far)

    build_tables()

    low_lanes = lane_ids((1, 1, LANES)) < LANES // 2
    lane_valid = jnp.where(low_lanes, not_tn, not_t0)
    last_lane = lane_ids((1, 1, LANES)) == LANES - 1
    first_lane = lane_ids((1, 1, LANES)) == 0

    def pack_time(block3, block0, low_ref, high_ref):
        high_ref[...] = jnp.where(low_lanes, pltpu.roll(block3[:, 32:64], 64, 2), block3[:, 0:32])
        low_ref[...] = jnp.where(low_lanes, block0[:, 0:32], pltpu.roll(block0[:, 32:64], 64, 2))

    def unpack_time(from_low, from_high):
        top = jnp.where(low_lanes, from_high, from_low)
        bottom = pltpu.roll(jnp.where(low_lanes, from_low, from_high), 64, 2)
        return jnp.concatenate([top, bottom], axis=1) * lane_valid

    def message(n, k):
        src, dst = {
            TO_HI: lambda: (X.at[n, 3, 0:4, 0:64, :], ril.at[n, 0:4, 0:64, :]),
            TO_LO: lambda: (X.at[n, 0, 0:4, 0:64, :], rih.at[n, 0:4, 0:64, :]),
            TO_JLO: lambda: (jlo.at[n], rjh.at[n]),
            TO_JHI: lambda: (jhi.at[n], rjl.at[n]),
            TO_THI: lambda: (thi.at[n], rtl.at[n]),
            TO_TLO: lambda: (tlo.at[n], rth.at[n]),
            E_IMJP: lambda: (jlo.at[n], eimjp.at[n]),
            E_IPJM: lambda: (jhi.at[n], eipjm.at[n]),
            E_IMTP: lambda: (clo.at[n], eimtp.at[n]),
            E_IPTM: lambda: (chi.at[n], eiptm.at[n]),
            E_JMTP: lambda: (jhi.at[n, 0], ejmtp.at[n]),
            E_JPTM: lambda: (jlo.at[n, 3], ejptm.at[n]),
        }[k]()
        return pltpu.make_async_remote_copy(
            src_ref=src, dst_ref=dst, send_sem=send_sem.at[n, k], recv_sem=recv_sem.at[n, k],
            device_id=at(*MESSAGES[k]), device_id_type=MESH,
        )

    def o_message(k):
        src, dst, off = ((ohi, rol, (0, 0, 1)), (olo, roh, (0, 0, -1)))[k]
        return pltpu.make_async_remote_copy(
            src_ref=src, dst_ref=dst, send_sem=osend.at[k], recv_sem=orecv.at[k],
            device_id=at(*off), device_id_type=MESH,
        )

    def sum_message(stage, d):
        if stage == 0:
            src, dst, ss, rs, off = part, r1.at[d], s1s, s1r, i_peers[d]
        else:
            src, dst, ss, rs, off = allsum, r2.at[d], s2s, s2r, p_peers[d]
        return pltpu.make_async_remote_copy(
            src_ref=src, dst_ref=dst, send_sem=ss.at[d], recv_sem=rs.at[d],
            device_id=at(*off), device_id_type=MESH,
        )

    def pack_and_send(n):
        model = X.at[0] if n == 0 else ms
        message(n, TO_HI).start()
        message(n, TO_LO).start()
        pack_time(model[:, 3, 0:64, :], model[:, 0, 0:64, :], tlo.at[n], thi.at[n])
        message(n, TO_THI).start()
        message(n, TO_TLO).start()
        for i in range(4):
            jlo[n, :, i : i + 1, :] = X[n, i, 0:4, 0:1, :]
            jhi[n, :, i : i + 1, :] = X[n, i, 0:4, 63:64, :]
        message(n, TO_JLO).start()
        message(n, TO_JHI).start()
        message(n, E_IMJP).start()
        message(n, E_IPJM).start()
        message(n, E_JMTP).start()
        message(n, E_JPTM).start()
        ids = lane_ids((8, LANES))
        low = X[n, 3, 0, 0:8, :]
        high = pltpu.roll(X[n, 0, 3, 0:8, :], 1, 1)
        for k in range(1, 8):
            low = jnp.where(ids == k, pltpu.roll(X[n, 3, 0, 8 * k : 8 * k + 8, :], k, 1), low)
            high = jnp.where(ids == k, pltpu.roll(X[n, 0, 3, 8 * k : 8 * k + 8, :], k + 1, 1), high)
        clo[n] = low
        chi[n] = high
        message(n, E_IMTP).start()
        message(n, E_IPTM).start()

    def receive(n):
        for k in MESSAGES:
            message(n, k).wait_recv()
        halo = unpack_time(rtl[n], rth[n])
        if n == 0:
            X[n, :, 4, 0:64, :] = halo
        else:
            X[n, :, 4, 0:64, :] = 2.0 * halo - mc[...]
        mc[...] = halo
        for i in range(4):
            X[n, i, 0:4, 64:65, :] = rjh[n, :, i : i + 1, :] * not_jn
            X[n, i, 4, 64:65, :] = ejptm[n, i : i + 1, :] * not_jn
        ril[n, 0:4, 64:65, :] = eimjp[n, :, 3:4, :] * not_jn
        low = eimtp[n] * not_tn
        high = eiptm[n] * not_t0
        for k in range(8):
            rows = slice(8 * k, 8 * k + 8)
            ril[n, 4, rows, :] = low if k == 0 else pltpu.roll(low, LANES - k, 1)
            rih[n, 4, rows, :] = pltpu.roll(high, LANES - 1 - k, 1)

    def lhs(blocks):
        pieces = [split(block.reshape(4 * 64, LANES)) for block in blocks]
        order = ((0, 1, 2, 4), (2, 3, 4, 1))
        return [
            jnp.concatenate([pieces[b][part_of] for part_of in (0, 1, 0) for b in which], axis=1)
            for which in order
        ]

    def halves(operands, tables):
        return [jnp.dot(x, t[...], preferred_element_type=F32) for x, t in zip(operands, tables)]

    def residual_sum(n, operands):
        total = jnp.zeros((8, LANES), F32)
        for half, value in enumerate(halves(operands, (tG, tG))):
            for b in range(2):
                e = value[:, b * LANES : (b + 1) * LANES] - obs[:, 2 * half + b].reshape(4 * 64, LANES)
                total = total + jnp.sum((e * e).reshape(4 * 8, 8, LANES), axis=0)
        row = lax.broadcasted_iota(jnp.int32, (8, LANES), 0)
        line = jnp.sum(total, axis=0, keepdims=True)
        if n == 0:
            part[...] = jnp.where(row == n, line, 0.0)
        else:
            part[...] = jnp.where(row == n, line, part[...])

    def put(ref, values):
        for half, value in enumerate(values):
            for b in range(2):
                ref[:, 2 * half + b] = value[:, b * LANES : (b + 1) * LANES].reshape(4, 64, LANES)

    def shrink(q0, q1, q2):
        scale = jnp.minimum(1.0, tv_weight * lax.rsqrt(q0 * q0 + q1 * q1 + q2 * q2))
        return q0 * scale, q1 * scale, q2 * scale

    def next_sample(x):
        moved = pltpu.roll(x, LANES - 1, 2)
        ahead = jnp.concatenate([moved[1:], moved[:1]], axis=0)
        return jnp.where(last_lane, ahead, moved)

    def trial(old, new, x):
        step = sigma_step * (new - x)
        return step if old is None else old + step

    def dual_below(n):
        def chunk(k, carry):
            rows = pl.ds(k * ROWS, ROWS)
            x5 = ril[n, :, rows, :]
            x = x5[0:4]
            xt = next_sample(x5)[0:4]
            xj = ril[n, 0:4, pl.ds(k * ROWS + 1, ROWS), :]
            xi = X[n, 0, 0:4, rows, :]
            old = [None] * 3 if n == 0 else [pm[c, :, rows, :] for c in range(3)]
            p0, p1, p2 = shrink(trial(old[0], xi, x), trial(old[1], xj, x), trial(old[2], xt, x))
            pm[0, :, rows, :] = p0 * not_i0
            pm[1, :, rows, :] = p1
            pm[2, :, rows, :] = p2
            return carry

        lax.fori_loop(0, 64 // ROWS, chunk, 0, unroll=True)

    def dual_before(n):
        row = lax.broadcasted_iota(jnp.int32, (1, 8, LANES), 1)
        above = pltpu.roll(eipjm[n], 4, 1) * not_in
        x = jnp.where(row < 4, rjl[n], above)
        x5 = jnp.concatenate([x, (ejmtp[n] * not_tn)[None]], axis=0)
        xt = next_sample(x5)[0:4]
        xi = pltpu.roll(x, 7, 1)
        xj = jlo[n]
        old = [None] * 3 if n == 0 else [pj[c] for c in range(3)]
        p0, p1, p2 = shrink(trial(old[0], xi, x), trial(old[1], xj, x), trial(old[2], xt, x))
        pj[0] = p0
        pj[1] = p1
        pj[2] = p2
        p1 = p1 * not_j0
        for i in range(4):
            pd1[i, 0:4, 7:8, :] = p1[:, i : i + 1, :]

    def layer(n, i):
        last = n == ITERS - 1

        def chunk(k, carry):
            rows = pl.ds(k * ROWS, ROWS)
            x = X[n, i, :, rows, :]
            xj = X[n, i, :, pl.ds(k * ROWS + 1, ROWS), :]
            xi = X[n, i + 1, :, rows, :] if i < 3 else rih[n, :, rows, :] * not_in
            xt = next_sample(x)
            shifted = pl.ds(k * ROWS + 8, ROWS)
            if n == 0:
                old = [None] * 3
            else:
                old = [pd0[i, :, rows, :], pd1[i, :, shifted, :], pd2[i, :, rows, :]]
            p0, p1, p2 = shrink(trial(old[0], xi, x), trial(old[1], xj, x), trial(old[2], xt, x))
            pd1[i, :, shifted, :] = p1
            pd0[i, :, rows, :] = p0
            if last:
                for b in range(4):
                    cols = pl.ds(b * LANES, LANES)
                    dout[0, i, rows, cols] = p0[b]
                    dout[1, i, rows, cols] = p1[b]
                    dout[2, i, rows, cols] = p2[b]
            else:
                pd2[i, :, rows, :] = p2
            before0 = pm[0, :, rows, :] if i == 0 else pd0[i - 1, 0:4, rows, :]
            before1 = pd1[i, 0:4, pl.ds(k * ROWS + 7, ROWS), :]
            moved = pltpu.roll(p2, 1, 2)
            behind = jnp.concatenate([moved[4:5] * not_t0, moved[0:3]], axis=0)
            before2 = jnp.where(first_lane, behind, moved[0:4])
            tv_term = (before0 - p0[0:4]) + (before1 - p1[0:4]) + (before2 - p2[0:4])
            model = x[0:4] if n == 0 else ms[i, :, rows, :]
            updated = model - tau_step * ((am[i, :, rows, :] - grad[i, :, rows, :]) + tv_term)
            if last:
                for b in range(4):
                    mout[i, rows, pl.ds(b * LANES, LANES)] = updated[b]
            else:
                ms[i, :, rows, :] = updated
                X[n + 1, i, 0:4, rows, :] = 2.0 * updated - model
            return carry

        lax.fori_loop(0, 64 // ROWS, chunk, 0, unroll=True)

    for load in loads:
        load.wait()
    pl.semaphore_wait(barrier, len(friends))
    pack_and_send(0)
    pack_time(obs[:, 3], obs[:, 0], olo, ohi)
    o_message(0).start()
    o_message(1).start()

    for n in range(ITERS):
        receive(n)
        model = X.at[0] if n == 0 else ms
        operands = lhs([model[:, b, 0:64, :] for b in range(4)] + [mc[...]])
        residual_sum(n, operands)
        if n == ITERS - 1:
            for d in range(len(i_peers)):
                sum_message(0, d).start()
        put(am, halves(operands, (tA0, tA1)))
        if n == 0:
            o_message(0).wait_recv()
            o_message(1).wait_recv()
            halo = unpack_time(rol[...], roh[...])
            put(grad, halves(lhs([obs[:, b] for b in range(4)] + [halo]), (tB, tB)))
        dual_below(n)
        dual_before(n)
        if n == ITERS - 1:
            total = part[...]
            for d in range(len(i_peers)):
                sum_message(0, d).wait_recv()
                total = total + r1[d]
            allsum[...] = total
            for d in range(len(p_peers)):
                sum_message(1, d).start()
        for i in range(4):
            layer(n, i)
        if n < ITERS - 1:
            pack_and_send(n + 1)

    total = allsum[...]
    for d in range(len(p_peers)):
        sum_message(1, d).wait_recv()
        total = total + r2[d]
    cells = 4 * 64 * 512 * n_i * n_j * n_t
    for n in range(ITERS):
        misf[n] = jnp.sum(total[n : n + 1, :]) * (1.0 / cells)

    for n in range(ITERS):
        for k in MESSAGES:
            message(n, k).wait_send()
    o_message(0).wait_send()
    o_message(1).wait_send()
    for d in range(len(i_peers)):
        sum_message(0, d).wait_send()
    for d in range(len(p_peers)):
        sum_message(1, d).wait_send()


def shards(n_inline, n_plane, observed, start_model, wavelet):
    dma = pltpu.SemaphoreType.DMA
    v = lambda *shape: pltpu.VMEM(shape, F32)
    scratch = [
        v(ITERS, 4, 5, 72, LANES),
        v(4, 4, 64, LANES),
        v(4, 4, 64, LANES),
        v(4, 4, 64, LANES),
        v(4, 4, 64, LANES),
        v(4, 64, LANES),
        v(ITERS, 5, 72, LANES),
        v(ITERS, 5, 64, LANES),
        v(ITERS, 4, 8, LANES),
        v(ITERS, 4, 8, LANES),
        v(ITERS, 4, 32, LANES),
        v(ITERS, 4, 32, LANES),
        v(4, 32, LANES),
        v(4, 32, LANES),
        v(ITERS, 4, 8, LANES),
        v(ITERS, 4, 8, LANES),
        v(ITERS, 8, LANES),
        v(ITERS, 8, LANES),
        v(ITERS, 8, LANES),
        v(ITERS, 8, LANES),
        v(ITERS, 4, 8, LANES),
        v(ITERS, 4, 8, LANES),
        v(ITERS, 4, 32, LANES),
        v(ITERS, 4, 32, LANES),
        v(4, 32, LANES),
        v(4, 32, LANES),
        v(ITERS, 8, LANES),
        v(ITERS, 8, LANES),
        v(4, 5, 64, LANES),
        v(4, 5, 72, LANES),
        v(4, 5, 64, LANES),
        v(3, 4, 64, LANES),
        v(3, 4, 8, LANES),
        v(8, LANES),
        v(8, LANES),
        v(n_inline - 1, 8, LANES),
        v(n_plane - 1, 8, LANES),
        pltpu.VMEM((6 * TILE, TILE), BF16),
        pltpu.VMEM((6 * TILE, TILE), BF16),
        pltpu.VMEM((6 * TILE, TILE), BF16),
        pltpu.VMEM((6 * TILE, TILE), BF16),
        dma((8,)),
        dma((ITERS, 12)),
        dma((ITERS, 12)),
        dma((2,)),
        dma((2,)),
        dma((n_inline - 1,)),
        dma((n_inline - 1,)),
        dma((n_plane - 1,)),
        dma((n_plane - 1,)),
    ]
    model, dual, misfits = pl.pallas_call(
        kernel,
        out_shape=(
            jax.ShapeDtypeStruct((4, 64, 512), F32),
            jax.ShapeDtypeStruct((3, 4, 64, 512), F32),
            jax.ShapeDtypeStruct((ITERS,), F32),
        ),
        in_specs=[
            pl.BlockSpec(memory_space=pl.ANY),
            pl.BlockSpec(memory_space=pl.ANY),
            pl.BlockSpec(memory_space=pltpu.SMEM),
        ],
        out_specs=(
            pl.BlockSpec(memory_space=pltpu.VMEM),
            pl.BlockSpec(memory_space=pltpu.VMEM),
            pl.BlockSpec(memory_space=pltpu.SMEM),
        ),
        scratch_shapes=scratch,
        compiler_params=pltpu.CompilerParams(
            collective_id=0, has_side_effects=True, vmem_limit_bytes=40 * 1024 * 1024
        ),
    )(observed, start_model, wavelet)
    return model, dual, misfits


def solution(mesh):
    sizes = dict(mesh.shape)
    body = functools.partial(shards, sizes["inline"], sizes["xline"] * sizes["tm"])
    in_specs = (P("inline", "xline", "tm"), P("inline", "xline", "tm"), P())
    out_specs = (P("inline", "xline", "tm"), P(None, "inline", "xline", "tm"), P())
    return jax.shard_map(body, mesh=mesh, in_specs=in_specs, out_specs=out_specs, check_vma=False)
```

```python
import functools

import jax
import jax.numpy as jnp
from jax import lax
from jax.experimental import pallas as pl
from jax.experimental.pallas import tpu as pltpu
from jax.sharding import PartitionSpec as P

TAPS = 64
ITERS = 4
LANES = 128
TILE = 256
ROWS = 16
MESH = pl.DeviceIdType.MESH
F32 = jnp.float32
BF16 = jnp.bfloat16

tau_step = 0.1
sigma_step = 0.5
tv_weight = 1.0
x_scale = tau_step * sigma_step

TO_HI, TO_LO, TO_JLO, TO_JHI, TO_THI, TO_TLO, E_IMJP, E_IPJM, E_IMTP, E_IPTM, E_JMTP, E_JPTM = range(12)
MESSAGES = {
    TO_HI: (1, 0, 0),
    TO_LO: (-1, 0, 0),
    TO_JLO: (0, -1, 0),
    TO_JHI: (0, 1, 0),
    TO_THI: (0, 0, 1),
    TO_TLO: (0, 0, -1),
    E_IMJP: (1, -1, 0),
    E_IPJM: (-1, 1, 0),
    E_IMTP: (1, 0, -1),
    E_IPTM: (-1, 0, 1),
    E_JMTP: (0, 1, -1),
    E_JPTM: (0, -1, 1),
}


def split(x):
    hi = x.astype(BF16)
    lo = (x - hi.astype(F32)).astype(BF16)
    return hi, lo


def lane_ids(shape):
    return lax.broadcasted_iota(jnp.int32, shape, len(shape) - 1)


def circulant(row):
    sub = lax.broadcasted_iota(jnp.int32, (8, TILE), 0)
    first = row
    for s in range(1, 8):
        first = jnp.where(sub == s, pltpu.roll(row, s, 1), first)
    return jnp.concatenate([first] + [pltpu.roll(first, 8 * g, 1) for g in range(1, TILE // 8)], axis=0)


def dot32(a, b):
    return jnp.dot(a, b, preferred_element_type=F32, precision=lax.Precision.HIGHEST)


def kernel(
    obs_hbm, start_hbm, wav_hbm, mout, dout, misf,
    X, ms, obs, grad, am, mc, ril, rih, rjl, rjh, rtl, rth, rol, roh,
    eimjp, eipjm, eimtp, eiptm, ejmtp, ejptm,
    jlo, jhi, tlo, thi, olo, ohi, clo, chi,
    pd0, pd1, pd2, pm, pj, part, allsum, r1, r2,
    tG, tA0, tA1, tB,
    wav, in_sem, send_sem, recv_sem, osend, orecv, s1s, s1r, s2s, s2r,
):
    n_i, n_j, n_t = lax.axis_size("inline"), lax.axis_size("xline"), lax.axis_size("tm")
    me_i, me_j, me_t = lax.axis_index("inline"), lax.axis_index("xline"), lax.axis_index("tm")

    def at(di, dj, dt):
        return (
            lax.rem(me_i + (di + n_i), n_i),
            lax.rem(me_j + (dj + n_j), n_j),
            lax.rem(me_t + (dt + n_t), n_t),
        )

    i_peers = sorted([(d, 0, 0) for d in range(1, n_i)], key=lambda o: -min(o[0], n_i - o[0]))
    p_peers = sorted(
        [(0, d // n_t, d % n_t) for d in range(1, n_j * n_t)],
        key=lambda o: -(min(o[1], n_j - o[1]) + min(o[2], n_t - o[2])),
    )
    near_by = [tuple(o % n for o, n in zip(off, (n_i, n_j, n_t))) for off in MESSAGES.values()]
    friends = list(dict.fromkeys(near_by + i_peers + p_peers))

    barrier = pltpu.get_barrier_semaphore()
    for off in friends:
        pl.semaphore_signal(barrier, inc=1, device_id=at(*off), device_id_type=MESH)

    loads = []
    for b in range(4):
        cols = pl.ds(b * LANES, LANES)
        loads.append(pltpu.make_async_copy(start_hbm.at[:, :, cols], ms.at[:, b], in_sem.at[b]))
    for b in range(4):
        cols = pl.ds(b * LANES, LANES)
        loads.append(pltpu.make_async_copy(obs_hbm.at[:, :, cols], obs.at[:, b], in_sem.at[4 + b]))
    loads.append(pltpu.make_async_copy(wav_hbm, wav, in_sem.at[8]))
    for load in loads:
        load.start()

    not_i0 = (me_i > 0).astype(F32)
    not_in = (me_i < n_i - 1).astype(F32)
    not_j0 = (me_j > 0).astype(F32)
    not_jn = (me_j < n_j - 1).astype(F32)
    not_t0 = (me_t > 0).astype(F32)
    not_tn = (me_t < n_t - 1).astype(F32)

    def build_tables():
        ids = lane_ids((8, TILE))
        w = jnp.zeros((8, TILE), F32)
        for k in range(TAPS):
            w = jnp.where(ids == k, wav[k], w)
        c = w - pltpu.roll(w, 1, 1)
        half = TAPS // 2 + 1
        circ_g = circulant(pltpu.roll(c, TILE - half, 1))
        rev = jnp.zeros((8, TILE), F32)
        for k in range(TAPS + 1):
            left = wav[k] if k < TAPS else 0.0
            right = wav[k - 1] if k > 0 else 0.0
            rev = jnp.where(ids == (half - k) % TILE, left - right, rev)
        circ_d = circulant(rev)
        r = lax.broadcasted_iota(jnp.int32, (TILE, TILE), 0)
        near = jnp.abs(r - lane_ids((TILE, TILE))) < LANES

        def store(table, rows, value):
            table[0, rows : rows + TILE, :], table[1, rows : rows + TILE, :] = split(value)

        g_far = jnp.where(near, 0.0, circ_g)
        d_far = jnp.where(near, 0.0, circ_d)
        store(tG, 0, jnp.where(near, circ_g, 0.0))
        store(tG, TILE, g_far)
        store(tB, 0, jnp.where(near, tau_step * circ_d, 0.0))
        store(tB, TILE, tau_step * d_far)
        circ_a = dot32(circ_g, tau_step * circ_d)
        edge = dot32(g_far, tau_step * d_far)
        a_near = jnp.where(near, circ_a, 0.0)
        a_far = jnp.where(near, 0.0, circ_a)
        store(tA0, 0, a_near - jnp.where(r < LANES, (1.0 - not_t0) * edge, 0.0))
        store(tA0, TILE, a_far)
        store(tA1, 0, a_near - jnp.where(r < LANES, 0.0, (1.0 - not_tn) * edge))
        store(tA1, TILE, a_far)


    low_lanes = lane_ids((1, 1, LANES)) < LANES // 2
    lane_valid = jnp.where(low_lanes, not_tn, not_t0)
    last_lane = lane_ids((1, 1, LANES)) == LANES - 1
    first_lane = lane_ids((1, 1, LANES)) == 0

    def pack_time(block3, block0, low_ref, high_ref):
        high_ref[...] = jnp.where(low_lanes, pltpu.roll(block3[:, 32:64], 64, 2), block3[:, 0:32])
        low_ref[...] = jnp.where(low_lanes, block0[:, 0:32], pltpu.roll(block0[:, 32:64], 64, 2))

    def unpack_time(from_low, from_high):
        top = jnp.where(low_lanes, from_high, from_low)
        bottom = pltpu.roll(jnp.where(low_lanes, from_low, from_high), 64, 2)
        return jnp.concatenate([top, bottom], axis=1) * lane_valid

    def message(n, k):
        src, dst = {
            TO_HI: lambda: (X.at[n, 3, 0:4, 0:64, :], ril.at[n, 0:4, 0:64, :]),
            TO_LO: lambda: (X.at[n, 0, 0:4, 0:64, :], rih.at[n, 0:4, 0:64, :]),
            TO_JLO: lambda: (jlo.at[n, :, 0:4, :], rjh.at[n, :, 0:4, :]),
            TO_JHI: lambda: (jhi.at[n, :, 0:4, :], rjl.at[n, :, 0:4, :]),
            TO_THI: lambda: (thi.at[n], rtl.at[n]),
            TO_TLO: lambda: (tlo.at[n], rth.at[n]),
            E_IMJP: lambda: (jlo.at[n, :, 3:4, :], eimjp.at[n, :, 3:4, :]),
            E_IPJM: lambda: (jhi.at[n, :, 0:1, :], eipjm.at[n, :, 0:1, :]),
            E_IMTP: lambda: (clo.at[n], eimtp.at[n]),
            E_IPTM: lambda: (chi.at[n], eiptm.at[n]),
            E_JMTP: lambda: (jhi.at[n, 0, 0:4], ejmtp.at[n, 0:4]),
            E_JPTM: lambda: (jlo.at[n, 3, 0:4], ejptm.at[n, 0:4]),
        }[k]()
        return pltpu.make_async_remote_copy(
            src_ref=src, dst_ref=dst, send_sem=send_sem.at[n, k], recv_sem=recv_sem.at[n, k],
            device_id=at(*MESSAGES[k]), device_id_type=MESH,
        )

    def o_message(k):
        src, dst, off = ((ohi, rol, (0, 0, 1)), (olo, roh, (0, 0, -1)))[k]
        return pltpu.make_async_remote_copy(
            src_ref=src, dst_ref=dst, send_sem=osend.at[k], recv_sem=orecv.at[k],
            device_id=at(*off), device_id_type=MESH,
        )

    def sum_message(stage, d):
        if stage == 0:
            src, dst, ss, rs, off = part, r1.at[d, 0:1], s1s, s1r, i_peers[d]
        else:
            src, dst, ss, rs, off = allsum, r2.at[d, 0:1], s2s, s2r, p_peers[d]
        return pltpu.make_async_remote_copy(
            src_ref=src, dst_ref=dst, send_sem=ss.at[d], recv_sem=rs.at[d],
            device_id=at(*off), device_id_type=MESH,
        )

    def pack(n):
        for i in range(4):
            jlo[n, :, i : i + 1, :] = X[n, i, 0:4, 0:1, :]
            jhi[n, :, i : i + 1, :] = X[n, i, 0:4, 63:64, :]
        ids = lane_ids((8, LANES))
        low = X[n, 3, 0, 0:8, :]
        high = pltpu.roll(X[n, 0, 3, 0:8, :], 1, 1)
        for k in range(1, 8):
            low = jnp.where(ids == k, pltpu.roll(X[n, 3, 0, 8 * k : 8 * k + 8, :], k, 1), low)
            high = jnp.where(ids == k, pltpu.roll(X[n, 0, 3, 8 * k : 8 * k + 8, :], k + 1, 1), high)
        clo[n] = low
        chi[n] = high

    def send(n):
        edges = (E_IMTP, E_IPTM, E_IMJP, E_IPJM, E_JMTP, E_JPTM)
        times = (TO_THI, TO_TLO)
        rest = (TO_HI, TO_LO)
        sides = (TO_JLO, TO_JHI)
        for k in times + edges + rest + sides if n == ITERS - 1 else edges + rest + times + sides:
            message(n, k).start()

    def receive_time(n):
        message(n, TO_THI).wait_recv()
        message(n, TO_TLO).wait_recv()
        halo = unpack_time(rtl[n], rth[n])
        if n == 0:
            X[n, :, 4, 0:64, :] = x_scale * halo
        else:
            X[n, :, 4, 0:64, :] = 2.0 * x_scale * halo - x_scale * mc[...]
        mc[...] = halo

    def receive_rest(n):
        for k in MESSAGES:
            if k not in (TO_THI, TO_TLO):
                message(n, k).wait_recv()
        for i in range(4):
            X[n, i, 0:4, 64:65, :] = rjh[n, :, i : i + 1, :] * not_jn
            X[n, i, 4, 64:65, :] = ejptm[n, i : i + 1, :] * not_jn
        ril[n, 0:4, 64:65, :] = eimjp[n, :, 3:4, :] * not_jn
        low = eimtp[n] * not_tn
        high = eiptm[n] * not_t0
        for k in range(8):
            rows = slice(8 * k, 8 * k + 8)
            ril[n, 4, rows, :] = low if k == 0 else pltpu.roll(low, LANES - k, 1)
            rih[n, 4, rows, :] = pltpu.roll(high, LANES - 1 - k, 1)

    def flat(block):
        return split(block.reshape(4 * 64, LANES))

    def join(pieces):
        return tuple(jnp.concatenate([p[k] for p in pieces], axis=1) for k in range(2))

    def product(x, table, start, stop):
        hi, lo = x
        dot = lambda a, b: jnp.dot(a, b, preferred_element_type=F32)
        return dot(hi, table[0, start:stop]) + dot(lo, table[0, start:stop]) + dot(hi, table[1, start:stop])

    def own_part(m, first, second):
        return [
            product(join([m[0], m[1], m[2]]), first, 0, 3 * LANES),
            product(join([m[2], m[3]]), second, 0, 2 * LANES) + product(m[1], second, 3 * LANES, 4 * LANES),
        ]

    def halo_part(c, first, second):
        return [product(c, first, 3 * LANES, 4 * LANES), product(c, second, 2 * LANES, 3 * LANES)]

    def residual_sum(n, values):
        total = jnp.zeros((8, LANES), F32)
        for half, value in enumerate(values):
            for b in range(2):
                e = value[:, b * LANES : (b + 1) * LANES] - obs[:, 2 * half + b].reshape(4 * 64, LANES)
                total = total + jnp.sum((e * e).reshape(4 * 8, 8, LANES), axis=0)
        line = jnp.sum(jnp.sum(total, axis=0, keepdims=True), axis=1, keepdims=True)
        lane = lane_ids((1, LANES))
        part[...] = jnp.where(lane == n, line, 0.0 if n == 0 else part[...])

    def put(ref, values, add=False):
        for half, value in enumerate(values):
            for b in range(2):
                v = value[:, b * LANES : (b + 1) * LANES].reshape(4, 64, LANES)
                ref[:, 2 * half + b] = ref[:, 2 * half + b] + v if add else v

    def shrink(q0, q1, q2):
        scale = jnp.minimum(1.0, tau_step * tv_weight * lax.rsqrt(q0 * q0 + q1 * q1 + q2 * q2))
        return q0 * scale, q1 * scale, q2 * scale

    def next_sample(x):
        moved = pltpu.roll(x, LANES - 1, 2)
        ahead = jnp.concatenate([moved[1:], moved[:1]], axis=0)
        return jnp.where(last_lane, ahead, moved)

    def trial(old, new, x):
        return new - x if old is None else old + (new - x)

    def dual_below(n):
        def chunk(k, carry):
            rows = pl.ds(k * ROWS, ROWS)
            x5 = ril[n, :, rows, :]
            x = x5[0:4]
            xt = next_sample(x5)[0:4]
            xj = ril[n, 0:4, pl.ds(k * ROWS + 1, ROWS), :]
            xi = X[n, 0, 0:4, rows, :]
            old = [None] * 3 if n == 0 else [pm[c, :, rows, :] for c in range(3)]
            p0, p1, p2 = shrink(trial(old[0], xi, x), trial(old[1], xj, x), trial(old[2], xt, x))
            pm[0, :, rows, :] = p0 * not_i0
            pm[1, :, rows, :] = p1
            pm[2, :, rows, :] = p2
            return carry

        lax.fori_loop(0, 64 // ROWS, chunk, 0, unroll=True)

    def dual_before(n):
        row = lax.broadcasted_iota(jnp.int32, (1, 8, LANES), 1)
        above = jnp.broadcast_to(eipjm[n, :, 0:1, :], (4, 8, LANES)) * not_in
        x = jnp.where(row < 4, rjl[n], above)
        x5 = jnp.concatenate([x, (ejmtp[n] * not_tn)[None]], axis=0)
        xt = next_sample(x5)[0:4]
        xi = pltpu.roll(x, 7, 1)
        xj = jlo[n]
        old = [None] * 3 if n == 0 else [pj[c] for c in range(3)]
        p0, p1, p2 = shrink(trial(old[0], xi, x), trial(old[1], xj, x), trial(old[2], xt, x))
        pj[0] = p0
        pj[1] = p1
        pj[2] = p2
        p1 = p1 * not_j0
        for i in range(4):
            pd1[i, 0:4, 7:8, :] = p1[:, i : i + 1, :]

    def dual_part(n, i, start, count, blocks):
        rows, shifted = pl.ds(start, count), pl.ds(start + 8, count)
        lo, hi = blocks
        cut = slice(lo, hi)
        x = X[n, i, cut, rows, :]
        after = X[n, i, hi % 5, rows, :][None]
        moved = pltpu.roll(x, LANES - 1, 2)
        ahead = jnp.concatenate([moved[1:], pltpu.roll(after, LANES - 1, 2)], axis=0)
        xt = jnp.where(last_lane, ahead, moved)
        xj = X[n, i, cut, pl.ds(start + 1, count), :]
        xi = X[n, i + 1, cut, rows, :] if i < 3 else rih[n, cut, rows, :] * not_in
        if n == 0:
            old = [None] * 3
        else:
            old = [pd0[i, cut, rows, :], pd1[i, cut, shifted, :], pd2[i, cut, rows, :]]
        p0, p1, p2 = shrink(trial(old[0], xi, x), trial(old[1], xj, x), trial(old[2], xt, x))
        pd0[i, cut, rows, :] = p0
        pd1[i, cut, shifted, :] = p1
        pd2[i, cut, rows, :] = p2
        if n == ITERS - 1:
            for b in range(lo, min(hi, 4)):
                cols = pl.ds(b * LANES, LANES)
                dout[0, i, rows, cols] = p0[b - lo] * (1.0 / tau_step)
                dout[1, i, rows, cols] = p1[b - lo] * (1.0 / tau_step)
                dout[2, i, rows, cols] = p2[b - lo] * (1.0 / tau_step)

    def dual_inside(n):
        for i in range(3):
            for start, count in ((0, 16), (16, 16), (32, 16), (48, 8)):
                dual_part(n, i, start, count, (0, 3))

    def dual_outside(n):
        dual_below(n)
        dual_before(n)
        for i in range(3):
            for start, count in ((0, 16), (16, 16), (32, 16), (48, 8)):
                dual_part(n, i, start, count, (3, 5))
            dual_part(n, i, 56, 8, (0, 5))
        for start in range(0, 64, 16):
            dual_part(n, 3, start, 16, (0, 5))

    def update(n, i):
        last = n == ITERS - 1

        def chunk(k, carry):
            rows = pl.ds(k * ROWS, ROWS)
            p2 = pd2[i, :, rows, :]
            before0 = pm[0, :, rows, :] if i == 0 else pd0[i - 1, 0:4, rows, :]
            before1 = pd1[i, 0:4, pl.ds(k * ROWS + 7, ROWS), :]
            moved = pltpu.roll(p2, 1, 2)
            behind = jnp.concatenate([moved[4:5] * not_t0, moved[0:3]], axis=0)
            before2 = jnp.where(first_lane, behind, moved[0:4])
            tv_term = before0 - pd0[i, 0:4, rows, :]
            tv_term = tv_term + (before1 - pd1[i, 0:4, pl.ds(k * ROWS + 8, ROWS), :])
            tv_term = tv_term + (before2 - p2[0:4])
            model = ms[i, :, rows, :]
            updated = model - ((am[i, :, rows, :] - grad[i, :, rows, :]) + tv_term)
            if last:
                for b in range(4):
                    mout[i, rows, pl.ds(b * LANES, LANES)] = updated[b]
            else:
                ms[i, :, rows, :] = updated
                X[n + 1, i, 0:4, rows, :] = (2.0 * x_scale) * updated - x_scale * model
            return carry

        lax.fori_loop(0, 64 // ROWS, chunk, 0, unroll=True)

    for load in loads[:4]:
        load.wait()
    X[0, :, 0:4, 0:64, :] = x_scale * ms[...]
    pack_time(ms[:, 3], ms[:, 0], tlo.at[0], thi.at[0])
    pack(0)
    pl.semaphore_wait(barrier, len(friends))
    send(0)
    for load in loads[4:]:
        load.wait()
    pack_time(obs[:, 3], obs[:, 0], olo, ohi)
    o_message(0).start()
    o_message(1).start()
    build_tables()
    put(grad, own_part([flat(obs[:, b]) for b in range(4)], tB, tB))

    kept = None
    for n in range(ITERS):
        if n > 0:
            residual_sum(n - 1, [a + b for a, b in zip(own_part(kept[0], tG, tG), halo_part(kept[1], tG, tG))])
        own = [flat(ms[:, b]) for b in range(4)]
        put(am, own_part(own, tA0, tA1))
        if n == ITERS - 1:
            last_own = own_part(own, tG, tG)
        dual_inside(n)
        receive_time(n)
        halo = flat(mc[...])
        kept = (own, halo)
        if n == ITERS - 1:
            residual_sum(n, [a + b for a, b in zip(last_own, halo_part(halo, tG, tG))])
            for d in range(len(i_peers)):
                sum_message(0, d).start()
        put(am, halo_part(halo, tA0, tA1), add=True)
        receive_rest(n)
        dual_outside(n)
        if n == 0:
            o_message(0).wait_recv()
            o_message(1).wait_recv()
            put(grad, halo_part(flat(unpack_time(rol[...], roh[...])), tB, tB), add=True)
        if n < ITERS - 1:
            for i in range(4):
                update(n, i)
            pack_time(ms[:, 3], ms[:, 0], tlo.at[n + 1], thi.at[n + 1])
            pack(n + 1)
            send(n + 1)
        else:
            for i in range(4):
                update(n, i)

    total = part[...]
    for d in range(len(i_peers)):
        sum_message(0, d).wait_recv()
        total = total + r1[d, 0:1]
    allsum[...] = total
    for d in range(len(p_peers)):
        sum_message(1, d).start()

    total = allsum[...]
    for d in range(len(p_peers)):
        sum_message(1, d).wait_recv()
        total = total + r2[d, 0:1]
    cells = 4 * 64 * 512 * n_i * n_j * n_t
    total = total * (1.0 / cells)
    for n in range(ITERS):
        misf[n] = total[0, n]

    for n in range(ITERS):
        for k in MESSAGES:
            message(n, k).wait_send()
    o_message(0).wait_send()
    o_message(1).wait_send()
    for d in range(len(i_peers)):
        sum_message(0, d).wait_send()
    for d in range(len(p_peers)):
        sum_message(1, d).wait_send()


def write_out(model, dual, misfits, model_out, dual_out, misfits_out, sem):
    pairs = ((model, model_out), (dual, dual_out), (misfits, misfits_out))
    copies = [pltpu.make_async_copy(src, dst, sem.at[k]) for k, (src, dst) in enumerate(pairs)]
    for copy in copies:
        copy.start()
    for copy in copies:
        copy.wait()


def shards(n_inline, n_plane, observed, start_model, wavelet):
    dma = pltpu.SemaphoreType.DMA
    v = lambda *shape: pltpu.VMEM(shape, F32)
    scratch = [
        v(ITERS, 4, 5, 72, LANES),
        v(4, 4, 64, LANES),
        v(4, 4, 64, LANES),
        v(4, 4, 64, LANES),
        v(4, 4, 64, LANES),
        v(4, 64, LANES),
        v(ITERS, 5, 72, LANES),
        v(ITERS, 5, 64, LANES),
        v(ITERS, 4, 8, LANES),
        v(ITERS, 4, 8, LANES),
        v(ITERS, 4, 32, LANES),
        v(ITERS, 4, 32, LANES),
        v(4, 32, LANES),
        v(4, 32, LANES),
        v(ITERS, 4, 8, LANES),
        v(ITERS, 4, 8, LANES),
        v(ITERS, 8, LANES),
        v(ITERS, 8, LANES),
        v(ITERS, 8, LANES),
        v(ITERS, 8, LANES),
        v(ITERS, 4, 8, LANES),
        v(ITERS, 4, 8, LANES),
        v(ITERS, 4, 32, LANES),
        v(ITERS, 4, 32, LANES),
        v(4, 32, LANES),
        v(4, 32, LANES),
        v(ITERS, 8, LANES),
        v(ITERS, 8, LANES),
        v(4, 5, 64, LANES),
        v(4, 5, 72, LANES),
        v(4, 5, 64, LANES),
        v(3, 4, 64, LANES),
        v(3, 4, 8, LANES),
        v(1, LANES),
        v(1, LANES),
        v(n_inline - 1, 8, LANES),
        v(n_plane - 1, 8, LANES),
        pltpu.VMEM((2, 2 * TILE, TILE), BF16),
        pltpu.VMEM((2, 2 * TILE, TILE), BF16),
        pltpu.VMEM((2, 2 * TILE, TILE), BF16),
        pltpu.VMEM((2, 2 * TILE, TILE), BF16),
        pltpu.SMEM((TAPS,), F32),
        dma((9,)),
        dma((ITERS, 12)),
        dma((ITERS, 12)),
        dma((2,)),
        dma((2,)),
        dma((n_inline - 1,)),
        dma((n_inline - 1,)),
        dma((n_plane - 1,)),
        dma((n_plane - 1,)),
    ]
    model, dual, misfits = pl.pallas_call(
        kernel,
        out_shape=(
            jax.ShapeDtypeStruct((4, 64, 512), F32),
            jax.ShapeDtypeStruct((3, 4, 64, 512), F32),
            jax.ShapeDtypeStruct((ITERS,), F32),
        ),
        in_specs=[
            pl.BlockSpec(memory_space=pl.ANY),
            pl.BlockSpec(memory_space=pl.ANY),
            pl.BlockSpec(memory_space=pl.ANY),
        ],
        out_specs=(
            pl.BlockSpec(memory_space=pltpu.VMEM),
            pl.BlockSpec(memory_space=pltpu.VMEM),
            pl.BlockSpec(memory_space=pltpu.SMEM),
        ),
        scratch_shapes=scratch,
        compiler_params=pltpu.CompilerParams(
            collective_id=0, has_side_effects=True, vmem_limit_bytes=40 * 1024 * 1024
        ),
    )(*[pltpu.with_memory_space_constraint(x, pltpu.HBM) for x in (observed, start_model, wavelet)])
    return pl.pallas_call(
        write_out,
        out_shape=(
            jax.ShapeDtypeStruct((4, 64, 512), F32),
            jax.ShapeDtypeStruct((3, 4, 64, 512), F32),
            jax.ShapeDtypeStruct((ITERS,), F32),
        ),
        in_specs=[pl.BlockSpec(memory_space=pltpu.VMEM)] * 3,
        out_specs=(pl.BlockSpec(memory_space=pl.ANY),) * 3,
        scratch_shapes=[pltpu.SemaphoreType.DMA((3,))],
    )(*[pltpu.with_memory_space_constraint(x, pltpu.VMEM) for x in (model, dual, misfits)])


def solution(mesh):
    sizes = dict(mesh.shape)
    body = functools.partial(shards, sizes["inline"], sizes["xline"] * sizes["tm"])
    in_specs = (P("inline", "xline", "tm"), P("inline", "xline", "tm"), P())
    out_specs = (P("inline", "xline", "tm"), P(None, "inline", "xline", "tm"), P())
    return jax.shard_map(body, mesh=mesh, in_specs=in_specs, out_specs=out_specs, check_vma=False)
```

```python
import functools

import jax
import jax.numpy as jnp
from jax import lax
from jax.experimental import pallas as pl
from jax.experimental.pallas import tpu as pltpu
from jax.sharding import PartitionSpec as P

TAPS = 64
ITERS = 4
LANES = 128
TILE = 256
ROWS = 16
MESH = pl.DeviceIdType.MESH
F32 = jnp.float32
BF16 = jnp.bfloat16

tau_step = 0.1
sigma_step = 0.5
tv_weight = 1.0
x_scale = tau_step * sigma_step

TO_HI, TO_LO, TO_JLO, TO_JHI, TO_THI, TO_TLO, E_IMJP, E_IPJM, E_IMTP, E_IPTM, E_JMTP, E_JPTM = range(12)
MESSAGES = {
    TO_HI: (1, 0, 0),
    TO_LO: (-1, 0, 0),
    TO_JLO: (0, -1, 0),
    TO_JHI: (0, 1, 0),
    TO_THI: (0, 0, 1),
    TO_TLO: (0, 0, -1),
    E_IMJP: (1, -1, 0),
    E_IPJM: (-1, 1, 0),
    E_IMTP: (1, 0, -1),
    E_IPTM: (-1, 0, 1),
    E_JMTP: (0, 1, -1),
    E_JPTM: (0, -1, 1),
}


def split(x):
    hi = x.astype(BF16)
    lo = (x - hi.astype(F32)).astype(BF16)
    return hi, lo


def lane_ids(shape):
    return lax.broadcasted_iota(jnp.int32, shape, len(shape) - 1)


def circulant(row):
    sub = lax.broadcasted_iota(jnp.int32, (8, TILE), 0)
    first = row
    for s in range(1, 8):
        first = jnp.where(sub == s, pltpu.roll(row, s, 1), first)
    return jnp.concatenate([first] + [pltpu.roll(first, 8 * g, 1) for g in range(1, TILE // 8)], axis=0)


def dot32(a, b):
    return jnp.dot(a, b, preferred_element_type=F32, precision=lax.Precision.HIGHEST)


def kernel(
    obs_hbm, start_hbm, wav_hbm, mout, dout, misf,
    X, ms, obs, grad, mnew, xnew, mc, ril, rih, rjl, rjh, rtl, rth, rol, roh,
    eimjp, eipjm, eimtp, eiptm, ejmtp, ejptm,
    jlo, jhi, tlo, thi, olo, ohi, clo, chi,
    pd0, pd1, pd2, pm, pj, part, allsum, r1, r2,
    tG, tA0, tA1, tB, hG, hA, hB,
    wav, in_sem, send_sem, recv_sem, osend, orecv, sum_sem,
):
    n_i, n_j, n_t = lax.axis_size("inline"), lax.axis_size("xline"), lax.axis_size("tm")
    me_i, me_j, me_t = lax.axis_index("inline"), lax.axis_index("xline"), lax.axis_index("tm")

    def at(di, dj, dt):
        return (
            lax.rem(me_i + (di + n_i), n_i),
            lax.rem(me_j + (dj + n_j), n_j),
            lax.rem(me_t + (dt + n_t), n_t),
        )

    i_peers = sorted([(d, 0, 0) for d in range(1, n_i)], key=lambda o: -min(o[0], n_i - o[0]))
    p_peers = sorted(
        [(0, d // n_t, d % n_t) for d in range(1, n_j * n_t)],
        key=lambda o: -(min(o[1], n_j - o[1]) + min(o[2], n_t - o[2])),
    )
    near_by = [tuple(o % n for o, n in zip(off, (n_i, n_j, n_t))) for off in reversed(MESSAGES.values())]
    friends = list(dict.fromkeys(near_by + i_peers + p_peers))

    barrier = pltpu.get_barrier_semaphore()
    for off in friends:
        pl.semaphore_signal(barrier, inc=1, device_id=at(*off), device_id_type=MESH)

    loads = []
    for b in range(4):
        cols = pl.ds(b * LANES, LANES)
        loads.append(pltpu.make_async_copy(start_hbm.at[:, :, cols], ms.at[:, b], in_sem.at[0]))
    for b in range(4):
        cols = pl.ds(b * LANES, LANES)
        loads.append(pltpu.make_async_copy(obs_hbm.at[:, :, cols], obs.at[:, b], in_sem.at[1]))
    loads.append(pltpu.make_async_copy(wav_hbm, wav, in_sem.at[2]))
    for load in loads:
        load.start()

    def all_of(ref, sem):
        return pltpu.make_async_copy(ref, ref, sem)

    not_i0 = (me_i > 0).astype(F32)
    not_in = (me_i < n_i - 1).astype(F32)
    not_j0 = (me_j > 0).astype(F32)
    not_jn = (me_j < n_j - 1).astype(F32)
    not_t0 = (me_t > 0).astype(F32)
    not_tn = (me_t < n_t - 1).astype(F32)

    def build_tables():
        ids = lane_ids((8, TILE))
        w = jnp.zeros((8, TILE), F32)
        for k in range(TAPS):
            w = jnp.where(ids == k, wav[k], w)
        c = w - pltpu.roll(w, 1, 1)
        half = TAPS // 2 + 1
        circ_g = circulant(pltpu.roll(c, TILE - half, 1))
        rev = jnp.zeros((8, TILE), F32)
        for k in range(TAPS + 1):
            left = wav[k] if k < TAPS else 0.0
            right = wav[k - 1] if k > 0 else 0.0
            rev = jnp.where(ids == (half - k) % TILE, left - right, rev)
        circ_d = circulant(rev)
        r = lax.broadcasted_iota(jnp.int32, (TILE, TILE), 0)
        near = jnp.abs(r - lane_ids((TILE, TILE))) < LANES

        def store(table, rows, value):
            table[0, rows : rows + TILE, :], table[1, rows : rows + TILE, :] = split(value)

        def store_halo(table, far):
            value = jnp.concatenate([far[LANES:TILE, 0:LANES], far[0:LANES, LANES:TILE]], axis=1)
            table[0], table[1] = split(value)

        g_far = jnp.where(near, 0.0, circ_g)
        d_far = jnp.where(near, 0.0, circ_d)
        store(tG, 0, jnp.where(near, circ_g, 0.0))
        store(tG, TILE, g_far)
        store(tB, 0, jnp.where(near, tau_step * circ_d, 0.0))
        store(tB, TILE, tau_step * d_far)
        store_halo(hG, g_far)
        store_halo(hB, tau_step * d_far)
        circ_a = dot32(circ_g, tau_step * circ_d)
        edge = dot32(g_far, tau_step * d_far)
        a_near = jnp.where(near, circ_a, 0.0)
        a_far = jnp.where(near, 0.0, circ_a)
        store(tA0, 0, a_near - jnp.where(r < LANES, (1.0 - not_t0) * edge, 0.0))
        store(tA0, TILE, a_far)
        store(tA1, 0, a_near - jnp.where(r < LANES, 0.0, (1.0 - not_tn) * edge))
        store(tA1, TILE, a_far)
        store_halo(hA, a_far)


    low_lanes = lane_ids((1, 1, LANES)) < LANES // 2
    lane_valid = jnp.where(low_lanes, not_tn, not_t0)
    last_lane = lane_ids((1, 1, LANES)) == LANES - 1
    first_lane = lane_ids((1, 1, LANES)) == 0

    def pack_time(block3, block0, low_ref, high_ref):
        high_ref[...] = jnp.where(low_lanes, pltpu.roll(block3[:, 32:64], 64, 2), block3[:, 0:32])
        low_ref[...] = jnp.where(low_lanes, block0[:, 0:32], pltpu.roll(block0[:, 32:64], 64, 2))

    def unpack_time(from_low, from_high):
        top = jnp.where(low_lanes, from_high, from_low)
        bottom = pltpu.roll(jnp.where(low_lanes, from_low, from_high), 64, 2)
        return jnp.concatenate([top, bottom], axis=1) * lane_valid

    def message(n, k):
        src, dst = {
            TO_HI: lambda: (X.at[n, 3, 0:4, 0:64, :], ril.at[n, 0:4, 0:64, :]),
            TO_LO: lambda: (X.at[n, 0, 0:4, 0:64, :], rih.at[n, 0:4, 0:64, :]),
            TO_JLO: lambda: (jlo.at[n, :, 0:4, :], rjh.at[n, :, 0:4, :]),
            TO_JHI: lambda: (jhi.at[n, :, 0:4, :], rjl.at[n, :, 0:4, :]),
            TO_THI: lambda: (thi.at[n], rtl.at[n]),
            TO_TLO: lambda: (tlo.at[n], rth.at[n]),
            E_IMJP: lambda: (jlo.at[n, :, 3:4, :], eimjp.at[n, :, 3:4, :]),
            E_IPJM: lambda: (jhi.at[n, :, 0:1, :], eipjm.at[n, :, 0:1, :]),
            E_IMTP: lambda: (clo.at[n], eimtp.at[n]),
            E_IPTM: lambda: (chi.at[n], eiptm.at[n]),
            E_JMTP: lambda: (jhi.at[n, 0, 0:4], ejmtp.at[n, 0:4]),
            E_JPTM: lambda: (jlo.at[n, 3, 0:4], ejptm.at[n, 0:4]),
        }[k]()
        return pltpu.make_async_remote_copy(
            src_ref=src, dst_ref=dst, send_sem=send_sem.at[k], recv_sem=recv_sem.at[n % 2, k],
            device_id=at(*MESSAGES[k]), device_id_type=MESH,
        )

    def o_message(k):
        src, dst, off = ((ohi, rol, (0, 0, 1)), (olo, roh, (0, 0, -1)))[k]
        return pltpu.make_async_remote_copy(
            src_ref=src, dst_ref=dst, send_sem=osend.at[k], recv_sem=orecv.at[k],
            device_id=at(*off), device_id_type=MESH,
        )

    def sum_message(stage, d):
        if stage == 0:
            src, dst, off = part, r1.at[d], i_peers[d]
        else:
            src, dst, off = allsum, r2.at[d], p_peers[d]
        return pltpu.make_async_remote_copy(
            src_ref=src, dst_ref=dst, send_sem=sum_sem.at[2 * stage], recv_sem=sum_sem.at[2 * stage + 1],
            device_id=at(*off), device_id_type=MESH,
        )

    def pack(n):
        for i in range(4):
            jlo[n, :, i : i + 1, :] = X[n, i, 0:4, 0:1, :]
            jhi[n, :, i : i + 1, :] = X[n, i, 0:4, 63:64, :]
        ids = lane_ids((8, LANES))
        low = X[n, 3, 0, 0:8, :]
        high = pltpu.roll(X[n, 0, 3, 0:8, :], 1, 1)
        for k in range(1, 8):
            low = jnp.where(ids == k, pltpu.roll(X[n, 3, 0, 8 * k : 8 * k + 8, :], k, 1), low)
            high = jnp.where(ids == k, pltpu.roll(X[n, 0, 3, 8 * k : 8 * k + 8, :], k + 1, 1), high)
        clo[n] = low
        chi[n] = high

    def start(n, kinds):
        for k in kinds:
            if n > 0:
                message(n - 1, k).wait_send()
            message(n, k).start()

    def send_time(n):
        pack_time(ms[:, 3], ms[:, 0], tlo.at[n], thi.at[n])
        start(n, (TO_THI, TO_TLO))

    def send(n):
        edges = (E_IMTP, E_IPTM, E_IMJP, E_IPJM, E_JMTP, E_JPTM)
        pack(n)
        start(n, edges + (TO_HI, TO_LO))
        if n < ITERS - 1:
            start(n, (TO_THI, TO_TLO))
        start(n, (TO_JLO, TO_JHI))

    def receive_time(n):
        message(n, TO_THI).wait_recv()
        message(n, TO_TLO).wait_recv()
        halo = unpack_time(rtl[n], rth[n])
        if n == 0:
            X[n, :, 4, 0:64, :] = x_scale * halo
        else:
            X[n, :, 4, 0:64, :] = 2.0 * x_scale * halo - x_scale * mc[...]
        mc[...] = halo

    def receive_rest(n):
        for k in MESSAGES:
            if k not in (TO_THI, TO_TLO):
                message(n, k).wait_recv()
        for i in range(4):
            X[n, i, 0:4, 64:65, :] = rjh[n, :, i : i + 1, :] * not_jn
            X[n, i, 4, 64:65, :] = ejptm[n, i : i + 1, :] * not_jn
        ril[n, 0:4, 64:65, :] = eimjp[n, :, 3:4, :] * not_jn
        low = eimtp[n] * not_tn
        high = eiptm[n] * not_t0
        for k in range(8):
            rows = slice(8 * k, 8 * k + 8)
            ril[n, 4, rows, :] = low if k == 0 else pltpu.roll(low, LANES - k, 1)
            rih[n, 4, rows, :] = pltpu.roll(high, LANES - 1 - k, 1)

    def flat(block):
        return split(block.reshape(4 * 64, LANES))

    def join(pieces):
        return tuple(jnp.concatenate([p[k] for p in pieces], axis=1) for k in range(2))

    def product(x, table, start, stop):
        hi, lo = x
        dot = lambda a, b: jnp.dot(a, b, preferred_element_type=F32)
        return dot(hi, table[0, start:stop]) + dot(lo, table[0, start:stop]) + dot(hi, table[1, start:stop])

    def own_part(m, first, second):
        return [
            product(join([m[0], m[1], m[2]]), first, 0, 3 * LANES),
            product(join([m[2], m[3]]), second, 0, 2 * LANES) + product(m[1], second, 3 * LANES, 4 * LANES),
        ]

    def halo_part(c, table):
        return product(c, table, 0, LANES)

    def put(ref, values):
        for half, value in enumerate(values):
            for b in range(2):
                ref[:, 2 * half + b] = value[:, b * LANES : (b + 1) * LANES].reshape(4, 64, LANES)

    def prepare(values):
        for half, value in enumerate(values):
            for b in range(2):
                k = 2 * half + b
                model = ms[:, k]
                new = model - (value[:, b * LANES : (b + 1) * LANES].reshape(4, 64, LANES) - grad[:, k])
                mnew[:, k] = new
                xnew[:, k] = (2.0 * x_scale) * new - x_scale * model

    def add_halo(value, sign):
        for k, b in enumerate((0, 3)):
            term = sign * value[:, k * LANES : (k + 1) * LANES].reshape(4, 64, LANES)
            mnew[:, b] = mnew[:, b] + term
            xnew[:, b] = xnew[:, b] + (2.0 * x_scale) * term

    def squares(e):
        return jnp.sum((e * e).reshape(4 * 8, 8, LANES), axis=0)

    def own_residual(m):
        left, right = own_part(m, tG, tG)
        blocks = [left[:, 0:LANES], left[:, LANES:TILE], right[:, 0:LANES], right[:, LANES:TILE]]
        e = [block - obs[:, b].reshape(4 * 64, LANES) for b, block in enumerate(blocks)]
        return e[0], e[3], squares(e[1]) + squares(e[2])

    def sum_up(n, own, c):
        first, last, total = own
        h = halo_part(c, hG)
        total = total + squares(first + h[:, 0:LANES]) + squares(last + h[:, LANES:TILE])
        line = jnp.sum(jnp.sum(total, axis=0, keepdims=True), axis=1, keepdims=True)
        lane = lane_ids((1, LANES))
        part[...] = jnp.where(lane == n, line, 0.0 if n == 0 else part[...])

    def shrink(q0, q1, q2):
        scale = jnp.minimum(1.0, tau_step * tv_weight * lax.rsqrt(q0 * q0 + q1 * q1 + q2 * q2))
        return q0 * scale, q1 * scale, q2 * scale

    def next_sample(x):
        moved = pltpu.roll(x, LANES - 1, 2)
        ahead = jnp.concatenate([moved[1:], moved[:1]], axis=0)
        return jnp.where(last_lane, ahead, moved)

    def trial(old, new, x):
        return new - x if old is None else old + (new - x)

    def dual_below(n):
        def chunk(k, carry):
            rows = pl.ds(k * ROWS, ROWS)
            x5 = ril[n, :, rows, :]
            x = x5[0:4]
            xt = next_sample(x5)[0:4]
            xj = ril[n, 0:4, pl.ds(k * ROWS + 1, ROWS), :]
            xi = X[n, 0, 0:4, rows, :]
            old = [None] * 3 if n == 0 else [pm[c, :, rows, :] for c in range(3)]
            p0, p1, p2 = shrink(trial(old[0], xi, x), trial(old[1], xj, x), trial(old[2], xt, x))
            pm[0, :, rows, :] = p0 * not_i0
            pm[1, :, rows, :] = p1
            pm[2, :, rows, :] = p2
            return carry

        lax.fori_loop(0, 64 // ROWS, chunk, 0, unroll=True)

    def dual_before(n):
        row = lax.broadcasted_iota(jnp.int32, (1, 8, LANES), 1)
        above = jnp.broadcast_to(eipjm[n, :, 0:1, :], (4, 8, LANES)) * not_in
        x = jnp.where(row < 4, rjl[n], above)
        x5 = jnp.concatenate([x, (ejmtp[n] * not_tn)[None]], axis=0)
        xt = next_sample(x5)[0:4]
        xi = pltpu.roll(x, 7, 1)
        xj = jlo[n]
        old = [None] * 3 if n == 0 else [pj[c] for c in range(3)]
        p0, p1, p2 = shrink(trial(old[0], xi, x), trial(old[1], xj, x), trial(old[2], xt, x))
        pj[0] = p0
        pj[1] = p1
        pj[2] = p2
        p1 = p1 * not_j0
        for i in range(4):
            pd1[i, 0:4, 7:8, :] = p1[:, i : i + 1, :]

    def dual_part(n, i, start, count, blocks):
        rows, shifted = pl.ds(start, count), pl.ds(start + 8, count)
        lo, hi = blocks
        cut = slice(lo, hi)
        x = X[n, i, cut, rows, :]
        after = X[n, i, hi % 5, rows, :][None]
        moved = pltpu.roll(x, LANES - 1, 2)
        ahead = jnp.concatenate([moved[1:], pltpu.roll(after, LANES - 1, 2)], axis=0)
        xt = jnp.where(last_lane, ahead, moved)
        xj = X[n, i, cut, pl.ds(start + 1, count), :]
        xi = X[n, i + 1, cut, rows, :] if i < 3 else rih[n, cut, rows, :] * not_in
        if n == 0:
            old = [None] * 3
        else:
            old = [pd0[i, cut, rows, :], pd1[i, cut, shifted, :], pd2[i, cut, rows, :]]
        p0, p1, p2 = shrink(trial(old[0], xi, x), trial(old[1], xj, x), trial(old[2], xt, x))
        pd0[i, cut, rows, :] = p0
        pd1[i, cut, shifted, :] = p1
        pd2[i, cut, rows, :] = p2
        if n == ITERS - 1:
            for b in range(lo, min(hi, 4)):
                cols = pl.ds(b * LANES, LANES)
                dout[0, i, rows, cols] = p0[b - lo] * (1.0 / tau_step)
                dout[1, i, rows, cols] = p1[b - lo] * (1.0 / tau_step)
                dout[2, i, rows, cols] = p2[b - lo] * (1.0 / tau_step)

    def dual_inside(n):
        for i in range(3):
            for start, count in ((0, 16), (16, 16), (32, 16), (48, 8)):
                dual_part(n, i, start, count, (0, 3))

    def dual_outside(n):
        dual_below(n)
        dual_before(n)
        for i in range(3):
            for start, count in ((0, 16), (16, 16), (32, 16), (48, 8)):
                dual_part(n, i, start, count, (3, 5))
            dual_part(n, i, 56, 8, (0, 5))
        for start in range(0, 64, 16):
            dual_part(n, 3, start, 16, (0, 5))

    def update(n, i, blocks):
        last = n == ITERS - 1
        lo, hi = blocks

        def chunk(k, carry):
            rows = pl.ds(k * ROWS, ROWS)
            cut = slice(lo, hi)
            p2 = pd2[i, cut, rows, :]
            ahead = pd2[i, (lo - 1) % 5, rows, :][None]
            if lo == 0:
                ahead = ahead * not_t0
            moved = pltpu.roll(p2, 1, 2)
            behind = pltpu.roll(ahead, 1, 2)
            if hi - lo > 1:
                behind = jnp.concatenate([behind, moved[:-1]], axis=0)
            before0 = pm[0, cut, rows, :] if i == 0 else pd0[i - 1, cut, rows, :]
            before1 = pd1[i, cut, pl.ds(k * ROWS + 7, ROWS), :]
            tv_term = before0 - pd0[i, cut, rows, :]
            tv_term = tv_term + (before1 - pd1[i, cut, pl.ds(k * ROWS + 8, ROWS), :])
            tv_term = tv_term + (jnp.where(first_lane, behind, moved) - p2)
            updated = mnew[i, cut, rows, :] - tv_term
            if last:
                for b in range(lo, hi):
                    mout[i, rows, pl.ds(b * LANES, LANES)] = updated[b - lo]
            else:
                ms[i, cut, rows, :] = updated
                X[n + 1, i, cut, rows, :] = xnew[i, cut, rows, :] - (2.0 * x_scale) * tv_term
            return carry

        lax.fori_loop(0, 64 // ROWS, chunk, 0, unroll=True)

    all_of(ms, in_sem.at[0]).wait()
    X[0, :, 0:4, 0:64, :] = x_scale * ms[...]
    pack_time(ms[:, 3], ms[:, 0], tlo.at[0], thi.at[0])
    pl.semaphore_wait(barrier, len(friends))
    send(0)
    all_of(obs, in_sem.at[1]).wait()
    loads[8].wait()
    pack_time(obs[:, 3], obs[:, 0], olo, ohi)
    o_message(0).start()
    o_message(1).start()
    build_tables()
    put(grad, own_part([flat(obs[:, b]) for b in range(4)], tB, tB))

    kept = None
    for n in range(ITERS):
        if n > 0:
            sum_up(n - 1, own_residual(kept[0]), kept[1])
        own = [flat(ms[:, b]) for b in range(4)]
        prepare(own_part(own, tA0, tA1))
        dual_inside(n)
        if n == ITERS - 1:
            last = own_residual(own)
            receive_time(n)
            halo = flat(mc[...])
            sum_up(n, last, halo)
            for d in range(len(i_peers)):
                sum_message(0, d).start()
            receive_rest(n)
        else:
            receive_time(n)
            receive_rest(n)
            halo = flat(mc[...])
            kept = (own, halo)
        add_halo(halo_part(halo, hA), -1.0)
        dual_outside(n)
        if n == 0:
            o_message(0).wait_recv()
            o_message(1).wait_recv()
            value = halo_part(flat(unpack_time(rol[...], roh[...])), hB)
            add_halo(value, 1.0)
            for k, b in enumerate((0, 3)):
                grad[:, b] = grad[:, b] + value[:, k * LANES : (k + 1) * LANES].reshape(4, 64, LANES)
        if n == ITERS - 2:
            for i in range(4):
                update(n, i, (0, 1))
                update(n, i, (3, 4))
            send_time(n + 1)
            for i in range(4):
                update(n, i, (1, 3))
            send(n + 1)
        else:
            for i in range(4):
                update(n, i, (0, 4))
            if n < ITERS - 1:
                pack_time(ms[:, 3], ms[:, 0], tlo.at[n + 1], thi.at[n + 1])
                send(n + 1)

    total = part[...]
    all_of(r1, sum_sem.at[1]).wait()
    for d in range(len(i_peers)):
        total = total + r1[d]
    allsum[...] = total
    for d in range(len(p_peers)):
        sum_message(1, d).start()

    total = allsum[...]
    all_of(r2, sum_sem.at[3]).wait()
    for d in range(len(p_peers)):
        total = total + r2[d]
    cells = 4 * 64 * 512 * n_i * n_j * n_t
    misf[...] = total * (1.0 / cells)

    for k in MESSAGES:
        message(ITERS - 1, k).wait_send()
    o_message(0).wait_send()
    o_message(1).wait_send()
    all_of(r1, sum_sem.at[0]).wait()
    all_of(r2, sum_sem.at[2]).wait()


def write_out(model, dual, misfits, model_out, dual_out, misfits_out, line, sem):
    pairs = ((dual, dual_out), (model, model_out), (line, misfits_out))
    copies = [pltpu.make_async_copy(src, dst, sem.at[k]) for k, (src, dst) in enumerate(pairs)]
    copies[0].start()
    copies[1].start()
    for n in range(ITERS):
        line[n] = misfits[0, n]
    copies[2].start()
    for copy in copies:
        copy.wait()


def shards(n_inline, n_plane, observed, start_model, wavelet):
    dma = pltpu.SemaphoreType.DMA
    v = lambda *shape: pltpu.VMEM(shape, F32)
    scratch = [
        v(ITERS, 4, 5, 72, LANES),
        v(4, 4, 64, LANES),
        v(4, 4, 64, LANES),
        v(4, 4, 64, LANES),
        v(4, 4, 64, LANES),
        v(4, 4, 64, LANES),
        v(4, 64, LANES),
        v(ITERS, 5, 72, LANES),
        v(ITERS, 5, 64, LANES),
        v(ITERS, 4, 8, LANES),
        v(ITERS, 4, 8, LANES),
        v(ITERS, 4, 32, LANES),
        v(ITERS, 4, 32, LANES),
        v(4, 32, LANES),
        v(4, 32, LANES),
        v(ITERS, 4, 8, LANES),
        v(ITERS, 4, 8, LANES),
        v(ITERS, 8, LANES),
        v(ITERS, 8, LANES),
        v(ITERS, 8, LANES),
        v(ITERS, 8, LANES),
        v(ITERS, 4, 8, LANES),
        v(ITERS, 4, 8, LANES),
        v(ITERS, 4, 32, LANES),
        v(ITERS, 4, 32, LANES),
        v(4, 32, LANES),
        v(4, 32, LANES),
        v(ITERS, 8, LANES),
        v(ITERS, 8, LANES),
        v(4, 5, 64, LANES),
        v(4, 5, 72, LANES),
        v(4, 5, 64, LANES),
        v(3, 4, 64, LANES),
        v(3, 4, 8, LANES),
        v(1, LANES),
        v(1, LANES),
        v(n_inline - 1, 1, LANES),
        v(n_plane - 1, 1, LANES),
        pltpu.VMEM((2, 2 * TILE, TILE), BF16),
        pltpu.VMEM((2, 2 * TILE, TILE), BF16),
        pltpu.VMEM((2, 2 * TILE, TILE), BF16),
        pltpu.VMEM((2, 2 * TILE, TILE), BF16),
        pltpu.VMEM((2, LANES, TILE), BF16),
        pltpu.VMEM((2, LANES, TILE), BF16),
        pltpu.VMEM((2, LANES, TILE), BF16),
        pltpu.SMEM((TAPS,), F32),
        dma((3,)),
        dma((12,)),
        dma((2, 12)),
        dma((2,)),
        dma((2,)),
        dma((4,)),
    ]
    model, dual, misfits = pl.pallas_call(
        kernel,
        out_shape=(
            pltpu.VMEM((4, 64, 512), F32),
            pltpu.VMEM((3, 4, 64, 512), F32),
            pltpu.VMEM((1, LANES), F32),
        ),
        in_specs=[
            pl.BlockSpec(memory_space=pl.ANY),
            pl.BlockSpec(memory_space=pl.ANY),
            pl.BlockSpec(memory_space=pl.ANY),
        ],
        out_specs=(
            pl.BlockSpec(memory_space=pltpu.VMEM),
            pl.BlockSpec(memory_space=pltpu.VMEM),
            pl.BlockSpec(memory_space=pltpu.VMEM),
        ),
        scratch_shapes=scratch,
        compiler_params=pltpu.CompilerParams(
            collective_id=0, has_side_effects=True, vmem_limit_bytes=40 * 1024 * 1024
        ),
    )(*[pltpu.with_memory_space_constraint(x, pltpu.HBM) for x in (observed, start_model, wavelet)])
    return pl.pallas_call(
        write_out,
        out_shape=(
            jax.ShapeDtypeStruct((4, 64, 512), F32),
            jax.ShapeDtypeStruct((3, 4, 64, 512), F32),
            jax.ShapeDtypeStruct((ITERS,), F32),
        ),
        in_specs=[pl.BlockSpec(memory_space=pltpu.VMEM)] * 3,
        out_specs=(pl.BlockSpec(memory_space=pl.ANY),) * 3,
        scratch_shapes=[pltpu.SMEM((ITERS,), F32), pltpu.SemaphoreType.DMA((3,))],
    )(*[pltpu.with_memory_space_constraint(x, pltpu.VMEM) for x in (model, dual, misfits)])


def solution(mesh):
    sizes = dict(mesh.shape)
    body = functools.partial(shards, sizes["inline"], sizes["xline"] * sizes["tm"])
    in_specs = (P("inline", "xline", "tm"), P("inline", "xline", "tm"), P())
    out_specs = (P("inline", "xline", "tm"), P(None, "inline", "xline", "tm"), P())
    return jax.shard_map(body, mesh=mesh, in_specs=in_specs, out_specs=out_specs, check_vma=False)
```

```python
import functools

import jax
import jax.numpy as jnp
from jax import lax
from jax.experimental import pallas as pl
from jax.experimental.pallas import tpu as pltpu
from jax.sharding import PartitionSpec as P

TAPS = 64
ITERS = 4
LANES = 128
TILE = 256
ROWS = 16
MESH = pl.DeviceIdType.MESH
F32 = jnp.float32
BF16 = jnp.bfloat16

tau_step = 0.1
sigma_step = 0.5
tv_weight = 1.0
x_scale = tau_step * sigma_step

TO_HI, TO_LO, TO_JLO, TO_JHI, TO_THI, TO_TLO, E_IMJP, E_IPJM, E_IMTP, E_IPTM, E_JMTP, E_JPTM = range(12)
MESSAGES = {
    TO_HI: (1, 0, 0),
    TO_LO: (-1, 0, 0),
    TO_JLO: (0, -1, 0),
    TO_JHI: (0, 1, 0),
    TO_THI: (0, 0, 1),
    TO_TLO: (0, 0, -1),
    E_IMJP: (1, -1, 0),
    E_IPJM: (-1, 1, 0),
    E_IMTP: (1, 0, -1),
    E_IPTM: (-1, 0, 1),
    E_JMTP: (0, 1, -1),
    E_JPTM: (0, -1, 1),
}


def split(x):
    hi = x.astype(BF16)
    lo = (x - hi.astype(F32)).astype(BF16)
    return hi, lo


def lane_ids(shape):
    return lax.broadcasted_iota(jnp.int32, shape, len(shape) - 1)


def circulant(row):
    sub = lax.broadcasted_iota(jnp.int32, (8, TILE), 0)
    first = row
    for s in range(1, 8):
        first = jnp.where(sub == s, pltpu.roll(row, s, 1), first)
    return jnp.concatenate([first] + [pltpu.roll(first, 8 * g, 1) for g in range(1, TILE // 8)], axis=0)


def dot32(a, b):
    return jnp.dot(a, b, preferred_element_type=F32, precision=lax.Precision.HIGHEST)


def kernel(
    obs_hbm, start_hbm, wav_hbm, mout, dout, misf,
    X, ms, obs, grad, mnew, xnew, mc, ril, rih, rjl, rjh, rtl, rth, rol, roh,
    eimjp, eipjm, eimtp, eiptm, ejmtp, ejptm,
    jlo, jhi, tlo, thi, olo, ohi, clo, chi,
    pd0, pd1, pd2, pm, pj, part, allsum, r1, r2,
    tG, tA0, tA1, tB, hG, hA, hB,
    wav, in_sem, send_sem, recv_sem, osend, orecv, sum_sem,
):
    n_i, n_j, n_t = lax.axis_size("inline"), lax.axis_size("xline"), lax.axis_size("tm")
    me_i, me_j, me_t = lax.axis_index("inline"), lax.axis_index("xline"), lax.axis_index("tm")

    def at(di, dj, dt):
        return (
            lax.rem(me_i + (di + n_i), n_i),
            lax.rem(me_j + (dj + n_j), n_j),
            lax.rem(me_t + (dt + n_t), n_t),
        )

    i_peers = sorted([(d, 0, 0) for d in range(1, n_i)], key=lambda o: -min(o[0], n_i - o[0]))
    p_peers = sorted(
        [(0, d // n_t, d % n_t) for d in range(1, n_j * n_t)],
        key=lambda o: -(min(o[1], n_j - o[1]) + min(o[2], n_t - o[2])),
    )
    near_by = [tuple(o % n for o, n in zip(off, (n_i, n_j, n_t))) for off in reversed(MESSAGES.values())]
    friends = list(dict.fromkeys(near_by + [(5, 0, 0), (n_i - 5, 0, 0)]))

    barrier = pltpu.get_barrier_semaphore()
    for off in friends:
        pl.semaphore_signal(barrier, inc=1, device_id=at(*off), device_id_type=MESH)

    loads = []
    for b in range(4):
        cols = pl.ds(b * LANES, LANES)
        loads.append(pltpu.make_async_copy(start_hbm.at[:, :, cols], ms.at[:, b], in_sem.at[0]))
    for b in range(4):
        cols = pl.ds(b * LANES, LANES)
        loads.append(pltpu.make_async_copy(obs_hbm.at[:, :, cols], obs.at[:, b], in_sem.at[1]))
    loads.append(pltpu.make_async_copy(wav_hbm, wav, in_sem.at[2]))
    for load in loads:
        load.start()

    def all_of(ref, sem):
        return pltpu.make_async_copy(ref, ref, sem)

    not_i0 = (me_i > 0).astype(F32)
    not_in = (me_i < n_i - 1).astype(F32)
    not_j0 = (me_j > 0).astype(F32)
    not_jn = (me_j < n_j - 1).astype(F32)
    not_t0 = (me_t > 0).astype(F32)
    not_tn = (me_t < n_t - 1).astype(F32)

    def build_tables():
        ids = lane_ids((8, TILE))
        w = jnp.zeros((8, TILE), F32)
        for k in range(TAPS):
            w = jnp.where(ids == k, wav[k], w)
        c = w - pltpu.roll(w, 1, 1)
        half = TAPS // 2 + 1
        circ_g = circulant(pltpu.roll(c, TILE - half, 1))
        rev = jnp.zeros((8, TILE), F32)
        for k in range(TAPS + 1):
            left = wav[k] if k < TAPS else 0.0
            right = wav[k - 1] if k > 0 else 0.0
            rev = jnp.where(ids == (half - k) % TILE, left - right, rev)
        circ_d = circulant(rev)
        r = lax.broadcasted_iota(jnp.int32, (TILE, TILE), 0)
        near = jnp.abs(r - lane_ids((TILE, TILE))) < LANES

        def store(table, rows, value):
            table[0, rows : rows + TILE, :], table[1, rows : rows + TILE, :] = split(value)

        def store_halo(table, far):
            value = jnp.concatenate([far[LANES:TILE, 0:LANES], far[0:LANES, LANES:TILE]], axis=1)
            table[0], table[1] = split(value)

        g_far = jnp.where(near, 0.0, circ_g)
        d_far = jnp.where(near, 0.0, circ_d)
        store(tG, 0, jnp.where(near, circ_g, 0.0))
        store(tG, TILE, g_far)
        store(tB, 0, jnp.where(near, tau_step * circ_d, 0.0))
        store(tB, TILE, tau_step * d_far)
        store_halo(hG, g_far)
        store_halo(hB, tau_step * d_far)
        circ_a = dot32(circ_g, tau_step * circ_d)
        edge = dot32(g_far, tau_step * d_far)
        a_near = jnp.where(near, circ_a, 0.0)
        a_far = jnp.where(near, 0.0, circ_a)
        store(tA0, 0, a_near - jnp.where(r < LANES, (1.0 - not_t0) * edge, 0.0))
        store(tA0, TILE, a_far)
        store(tA1, 0, a_near - jnp.where(r < LANES, 0.0, (1.0 - not_tn) * edge))
        store(tA1, TILE, a_far)
        store_halo(hA, a_far)


    low_lanes = lane_ids((1, 1, LANES)) < LANES // 2
    lane_valid = jnp.where(low_lanes, not_tn, not_t0)
    last_lane = lane_ids((1, 1, LANES)) == LANES - 1
    first_lane = lane_ids((1, 1, LANES)) == 0

    def pack_time(block3, block0, low_ref, high_ref):
        high_ref[...] = jnp.where(low_lanes, pltpu.roll(block3[:, 32:64], 64, 2), block3[:, 0:32])
        low_ref[...] = jnp.where(low_lanes, block0[:, 0:32], pltpu.roll(block0[:, 32:64], 64, 2))

    def unpack_time(from_low, from_high):
        top = jnp.where(low_lanes, from_high, from_low)
        bottom = pltpu.roll(jnp.where(low_lanes, from_low, from_high), 64, 2)
        return jnp.concatenate([top, bottom], axis=1) * lane_valid

    def message(n, k):
        src, dst = {
            TO_HI: lambda: (X.at[n, 3, 0:4, 0:64, :], ril.at[n, 0:4, 0:64, :]),
            TO_LO: lambda: (X.at[n, 0, 0:4, 0:64, :], rih.at[n, 0:4, 0:64, :]),
            TO_JLO: lambda: (jlo.at[n, :, 0:4, :], rjh.at[n, :, 0:4, :]),
            TO_JHI: lambda: (jhi.at[n, :, 0:4, :], rjl.at[n, :, 0:4, :]),
            TO_THI: lambda: (thi.at[n], rtl.at[n]),
            TO_TLO: lambda: (tlo.at[n], rth.at[n]),
            E_IMJP: lambda: (jlo.at[n, :, 3:4, :], eimjp.at[n, :, 3:4, :]),
            E_IPJM: lambda: (jhi.at[n, :, 0:1, :], eipjm.at[n, :, 0:1, :]),
            E_IMTP: lambda: (clo.at[n], eimtp.at[n]),
            E_IPTM: lambda: (chi.at[n], eiptm.at[n]),
            E_JMTP: lambda: (jhi.at[n, 0, 0:4], ejmtp.at[n, 0:4]),
            E_JPTM: lambda: (jlo.at[n, 3, 0:4], ejptm.at[n, 0:4]),
        }[k]()
        return pltpu.make_async_remote_copy(
            src_ref=src, dst_ref=dst, send_sem=send_sem.at[k], recv_sem=recv_sem.at[n % 2, k],
            device_id=at(*MESSAGES[k]), device_id_type=MESH,
        )

    def o_message(k):
        src, dst, off = ((ohi, rol, (0, 0, 1)), (olo, roh, (0, 0, -1)))[k]
        return pltpu.make_async_remote_copy(
            src_ref=src, dst_ref=dst, send_sem=osend.at[k], recv_sem=orecv.at[k],
            device_id=at(*off), device_id_type=MESH,
        )

    def sum_message(stage, d):
        if stage == 0:
            src, dst, off = part, r1.at[d], i_peers[d]
        else:
            src, dst, off = allsum, r2.at[d], p_peers[d]
        return pltpu.make_async_remote_copy(
            src_ref=src, dst_ref=dst, send_sem=sum_sem.at[2 * stage], recv_sem=sum_sem.at[2 * stage + 1],
            device_id=at(*off), device_id_type=MESH,
        )

    def pack(n):
        for i in range(4):
            jlo[n, :, i : i + 1, :] = X[n, i, 0:4, 0:1, :]
            jhi[n, :, i : i + 1, :] = X[n, i, 0:4, 63:64, :]
        ids = lane_ids((8, LANES))
        low = X[n, 3, 0, 0:8, :]
        high = pltpu.roll(X[n, 0, 3, 0:8, :], 1, 1)
        for k in range(1, 8):
            low = jnp.where(ids == k, pltpu.roll(X[n, 3, 0, 8 * k : 8 * k + 8, :], k, 1), low)
            high = jnp.where(ids == k, pltpu.roll(X[n, 0, 3, 8 * k : 8 * k + 8, :], k + 1, 1), high)
        clo[n] = low
        chi[n] = high

    def start(n, kinds):
        for k in kinds:
            if n > 0:
                message(n - 1, k).wait_send()
            message(n, k).start()

    def send_time(n):
        pack_time(ms[:, 3], ms[:, 0], tlo.at[n], thi.at[n])
        start(n, (TO_THI, TO_TLO))

    def send(n):
        edges = (E_IMTP, E_IPTM, E_IMJP, E_IPJM, E_JMTP, E_JPTM)
        pack(n)
        start(n, edges + (TO_HI, TO_LO))
        if n < ITERS - 1:
            start(n, (TO_THI, TO_TLO))
        start(n, (TO_JLO, TO_JHI))

    def receive_time(n):
        message(n, TO_THI).wait_recv()
        message(n, TO_TLO).wait_recv()
        halo = unpack_time(rtl[n], rth[n])
        if n == 0:
            X[n, :, 4, 0:64, :] = x_scale * halo
        else:
            X[n, :, 4, 0:64, :] = 2.0 * x_scale * halo - x_scale * mc[...]
        mc[...] = halo

    def receive_rest(n):
        for k in MESSAGES:
            if k not in (TO_THI, TO_TLO):
                message(n, k).wait_recv()
        for i in range(4):
            X[n, i, 0:4, 64:65, :] = rjh[n, :, i : i + 1, :] * not_jn
            X[n, i, 4, 64:65, :] = ejptm[n, i : i + 1, :] * not_jn
        ril[n, 0:4, 64:65, :] = eimjp[n, :, 3:4, :] * not_jn
        low = eimtp[n] * not_tn
        high = eiptm[n] * not_t0
        for k in range(8):
            rows = slice(8 * k, 8 * k + 8)
            ril[n, 4, rows, :] = low if k == 0 else pltpu.roll(low, LANES - k, 1)
            rih[n, 4, rows, :] = pltpu.roll(high, LANES - 1 - k, 1)

    def flat(block):
        return split(block.reshape(4 * 64, LANES))

    def join(pieces):
        return tuple(jnp.concatenate([p[k] for p in pieces], axis=1) for k in range(2))

    def product(x, table, start, stop):
        hi, lo = x
        dot = lambda a, b: jnp.dot(a, b, preferred_element_type=F32)
        return dot(hi, table[0, start:stop]) + dot(lo, table[0, start:stop]) + dot(hi, table[1, start:stop])

    def own_part(m, first, second):
        return [
            product(join([m[0], m[1], m[2]]), first, 0, 3 * LANES),
            product(join([m[2], m[3]]), second, 0, 2 * LANES) + product(m[1], second, 3 * LANES, 4 * LANES),
        ]

    def halo_part(c, table):
        return product(c, table, 0, LANES)

    def put(ref, values):
        for half, value in enumerate(values):
            for b in range(2):
                ref[:, 2 * half + b] = value[:, b * LANES : (b + 1) * LANES].reshape(4, 64, LANES)

    def prepare(values):
        for half, value in enumerate(values):
            for b in range(2):
                k = 2 * half + b
                model = ms[:, k]
                new = model - (value[:, b * LANES : (b + 1) * LANES].reshape(4, 64, LANES) - grad[:, k])
                mnew[:, k] = new
                xnew[:, k] = (2.0 * x_scale) * new - x_scale * model

    def add_halo(value, sign):
        for k, b in enumerate((0, 3)):
            term = sign * value[:, k * LANES : (k + 1) * LANES].reshape(4, 64, LANES)
            mnew[:, b] = mnew[:, b] + term
            xnew[:, b] = xnew[:, b] + (2.0 * x_scale) * term

    def squares(e):
        return jnp.sum((e * e).reshape(4 * 8, 8, LANES), axis=0)

    def own_residual(m):
        left, right = own_part(m, tG, tG)
        blocks = [left[:, 0:LANES], left[:, LANES:TILE], right[:, 0:LANES], right[:, LANES:TILE]]
        e = [block - obs[:, b].reshape(4 * 64, LANES) for b, block in enumerate(blocks)]
        return e[0], e[3], squares(e[1]) + squares(e[2])

    def sum_up(n, own, c):
        first, last, total = own
        h = halo_part(c, hG)
        total = total + squares(first + h[:, 0:LANES]) + squares(last + h[:, LANES:TILE])
        line = jnp.sum(jnp.sum(total, axis=0, keepdims=True), axis=1, keepdims=True)
        lane = lane_ids((1, LANES))
        part[...] = jnp.where(lane == n, line, 0.0 if n == 0 else part[...])

    def shrink(q0, q1, q2):
        scale = jnp.minimum(1.0, tau_step * tv_weight * lax.rsqrt(q0 * q0 + q1 * q1 + q2 * q2))
        return q0 * scale, q1 * scale, q2 * scale

    def next_sample(x):
        moved = pltpu.roll(x, LANES - 1, 2)
        ahead = jnp.concatenate([moved[1:], moved[:1]], axis=0)
        return jnp.where(last_lane, ahead, moved)

    def trial(old, new, x):
        return new - x if old is None else old + (new - x)

    def dual_below(n):
        def chunk(k, carry):
            rows = pl.ds(k * ROWS, ROWS)
            x5 = ril[n, :, rows, :]
            x = x5[0:4]
            xt = next_sample(x5)[0:4]
            xj = ril[n, 0:4, pl.ds(k * ROWS + 1, ROWS), :]
            xi = X[n, 0, 0:4, rows, :]
            old = [None] * 3 if n == 0 else [pm[c, :, rows, :] for c in range(3)]
            p0, p1, p2 = shrink(trial(old[0], xi, x), trial(old[1], xj, x), trial(old[2], xt, x))
            pm[0, :, rows, :] = p0 * not_i0
            pm[1, :, rows, :] = p1
            pm[2, :, rows, :] = p2
            return carry

        lax.fori_loop(0, 64 // ROWS, chunk, 0, unroll=True)

    def dual_before(n):
        row = lax.broadcasted_iota(jnp.int32, (1, 8, LANES), 1)
        above = jnp.broadcast_to(eipjm[n, :, 0:1, :], (4, 8, LANES)) * not_in
        x = jnp.where(row < 4, rjl[n], above)
        x5 = jnp.concatenate([x, (ejmtp[n] * not_tn)[None]], axis=0)
        xt = next_sample(x5)[0:4]
        xi = pltpu.roll(x, 7, 1)
        xj = jlo[n]
        old = [None] * 3 if n == 0 else [pj[c] for c in range(3)]
        p0, p1, p2 = shrink(trial(old[0], xi, x), trial(old[1], xj, x), trial(old[2], xt, x))
        pj[0] = p0
        pj[1] = p1
        pj[2] = p2
        p1 = p1 * not_j0
        for i in range(4):
            pd1[i, 0:4, 7:8, :] = p1[:, i : i + 1, :]

    def dual_part(n, i, start, count, blocks):
        rows, shifted = pl.ds(start, count), pl.ds(start + 8, count)
        lo, hi = blocks
        cut = slice(lo, hi)
        x = X[n, i, cut, rows, :]
        after = X[n, i, hi % 5, rows, :][None]
        moved = pltpu.roll(x, LANES - 1, 2)
        ahead = jnp.concatenate([moved[1:], pltpu.roll(after, LANES - 1, 2)], axis=0)
        xt = jnp.where(last_lane, ahead, moved)
        xj = X[n, i, cut, pl.ds(start + 1, count), :]
        xi = X[n, i + 1, cut, rows, :] if i < 3 else rih[n, cut, rows, :] * not_in
        if n == 0:
            old = [None] * 3
        else:
            old = [pd0[i, cut, rows, :], pd1[i, cut, shifted, :], pd2[i, cut, rows, :]]
        p0, p1, p2 = shrink(trial(old[0], xi, x), trial(old[1], xj, x), trial(old[2], xt, x))
        pd0[i, cut, rows, :] = p0
        pd1[i, cut, shifted, :] = p1
        pd2[i, cut, rows, :] = p2
        if n == ITERS - 1:
            for b in range(lo, min(hi, 4)):
                cols = pl.ds(b * LANES, LANES)
                dout[0, i, rows, cols] = p0[b - lo] * (1.0 / tau_step)
                dout[1, i, rows, cols] = p1[b - lo] * (1.0 / tau_step)
                dout[2, i, rows, cols] = p2[b - lo] * (1.0 / tau_step)

    def dual_inside(n):
        for i in range(3):
            for start, count in ((0, 16), (16, 16), (32, 16), (48, 8)):
                dual_part(n, i, start, count, (0, 3))

    def dual_outside(n):
        dual_below(n)
        dual_before(n)
        for i in range(3):
            for start, count in ((0, 16), (16, 16), (32, 16), (48, 8)):
                dual_part(n, i, start, count, (3, 5))
            dual_part(n, i, 56, 8, (0, 5))
        for start in range(0, 64, 16):
            dual_part(n, 3, start, 16, (0, 5))

    def update(n, i, blocks):
        last = n == ITERS - 1
        lo, hi = blocks

        def chunk(k, carry):
            rows = pl.ds(k * ROWS, ROWS)
            cut = slice(lo, hi)
            p2 = pd2[i, cut, rows, :]
            ahead = pd2[i, (lo - 1) % 5, rows, :][None]
            if lo == 0:
                ahead = ahead * not_t0
            moved = pltpu.roll(p2, 1, 2)
            behind = pltpu.roll(ahead, 1, 2)
            if hi - lo > 1:
                behind = jnp.concatenate([behind, moved[:-1]], axis=0)
            before0 = pm[0, cut, rows, :] if i == 0 else pd0[i - 1, cut, rows, :]
            before1 = pd1[i, cut, pl.ds(k * ROWS + 7, ROWS), :]
            tv_term = before0 - pd0[i, cut, rows, :]
            tv_term = tv_term + (before1 - pd1[i, cut, pl.ds(k * ROWS + 8, ROWS), :])
            tv_term = tv_term + (jnp.where(first_lane, behind, moved) - p2)
            updated = mnew[i, cut, rows, :] - tv_term
            if last:
                for b in range(lo, hi):
                    mout[i, rows, pl.ds(b * LANES, LANES)] = updated[b - lo]
            else:
                ms[i, cut, rows, :] = updated
                X[n + 1, i, cut, rows, :] = xnew[i, cut, rows, :] - (2.0 * x_scale) * tv_term
            return carry

        lax.fori_loop(0, 64 // ROWS, chunk, 0, unroll=True)

    all_of(ms, in_sem.at[0]).wait()
    X[0, :, 0:4, 0:64, :] = x_scale * ms[...]
    pack_time(ms[:, 3], ms[:, 0], tlo.at[0], thi.at[0])
    pl.semaphore_wait(barrier, len(friends))
    send(0)
    all_of(obs, in_sem.at[1]).wait()
    loads[8].wait()
    pack_time(obs[:, 3], obs[:, 0], olo, ohi)
    o_message(0).start()
    o_message(1).start()
    build_tables()
    put(grad, own_part([flat(obs[:, b]) for b in range(4)], tB, tB))

    kept = None
    for n in range(ITERS):
        if n > 0:
            sum_up(n - 1, own_residual(kept[0]), kept[1])
        own = [flat(ms[:, b]) for b in range(4)]
        prepare(own_part(own, tA0, tA1))
        dual_inside(n)
        if n == ITERS - 1:
            last = own_residual(own)
            receive_time(n)
            halo = flat(mc[...])
            sum_up(n, last, halo)
            for d in range(len(i_peers)):
                sum_message(0, d).start()
            receive_rest(n)
        else:
            receive_time(n)
            receive_rest(n)
            halo = flat(mc[...])
            kept = (own, halo)
        add_halo(halo_part(halo, hA), -1.0)
        dual_outside(n)
        if n == 0:
            o_message(0).wait_recv()
            o_message(1).wait_recv()
            value = halo_part(flat(unpack_time(rol[...], roh[...])), hB)
            add_halo(value, 1.0)
            for k, b in enumerate((0, 3)):
                grad[:, b] = grad[:, b] + value[:, k * LANES : (k + 1) * LANES].reshape(4, 64, LANES)
        if n == ITERS - 2:
            for i in range(4):
                update(n, i, (0, 1))
                update(n, i, (3, 4))
            send_time(n + 1)
            for i in range(4):
                update(n, i, (1, 3))
            send(n + 1)
        else:
            for i in range(4):
                update(n, i, (0, 4))
            if n < ITERS - 1:
                pack_time(ms[:, 3], ms[:, 0], tlo.at[n + 1], thi.at[n + 1])
                send(n + 1)

    total = part[...]
    all_of(r1, sum_sem.at[1]).wait()
    for d in range(len(i_peers)):
        total = total + r1[d]
    allsum[...] = total
    for d in range(len(p_peers)):
        sum_message(1, d).start()

    total = allsum[...]
    all_of(r2, sum_sem.at[3]).wait()
    for d in range(len(p_peers)):
        total = total + r2[d]
    cells = 4 * 64 * 512 * n_i * n_j * n_t
    misf[...] = total * (1.0 / cells)

    for k in MESSAGES:
        message(ITERS - 1, k).wait_send()
    o_message(0).wait_send()
    o_message(1).wait_send()
    all_of(r1, sum_sem.at[0]).wait()
    all_of(r2, sum_sem.at[2]).wait()


def write_out(model, dual, misfits, model_out, dual_out, misfits_out, line, sem):
    pairs = ((dual, dual_out), (model, model_out), (line, misfits_out))
    copies = [pltpu.make_async_copy(src, dst, sem.at[k]) for k, (src, dst) in enumerate(pairs)]
    copies[0].start()
    copies[1].start()
    for n in range(ITERS):
        line[n] = misfits[0, n]
    copies[2].start()
    for copy in copies:
        copy.wait()


def shards(n_inline, n_plane, observed, start_model, wavelet):
    dma = pltpu.SemaphoreType.DMA
    v = lambda *shape: pltpu.VMEM(shape, F32)
    scratch = [
        v(ITERS, 4, 5, 72, LANES),
        v(4, 4, 64, LANES),
        v(4, 4, 64, LANES),
        v(4, 4, 64, LANES),
        v(4, 4, 64, LANES),
        v(4, 4, 64, LANES),
        v(4, 64, LANES),
        v(ITERS, 5, 72, LANES),
        v(ITERS, 5, 64, LANES),
        v(ITERS, 4, 8, LANES),
        v(ITERS, 4, 8, LANES),
        v(ITERS, 4, 32, LANES),
        v(ITERS, 4, 32, LANES),
        v(4, 32, LANES),
        v(4, 32, LANES),
        v(ITERS, 4, 8, LANES),
        v(ITERS, 4, 8, LANES),
        v(ITERS, 8, LANES),
        v(ITERS, 8, LANES),
        v(ITERS, 8, LANES),
        v(ITERS, 8, LANES),
        v(ITERS, 4, 8, LANES),
        v(ITERS, 4, 8, LANES),
        v(ITERS, 4, 32, LANES),
        v(ITERS, 4, 32, LANES),
        v(4, 32, LANES),
        v(4, 32, LANES),
        v(ITERS, 8, LANES),
        v(ITERS, 8, LANES),
        v(4, 5, 64, LANES),
        v(4, 5, 72, LANES),
        v(4, 5, 64, LANES),
        v(3, 4, 64, LANES),
        v(3, 4, 8, LANES),
        v(1, LANES),
        v(1, LANES),
        v(n_inline - 1, 1, LANES),
        v(n_plane - 1, 1, LANES),
        pltpu.VMEM((2, 2 * TILE, TILE), BF16),
        pltpu.VMEM((2, 2 * TILE, TILE), BF16),
        pltpu.VMEM((2, 2 * TILE, TILE), BF16),
        pltpu.VMEM((2, 2 * TILE, TILE), BF16),
        pltpu.VMEM((2, LANES, TILE), BF16),
        pltpu.VMEM((2, LANES, TILE), BF16),
        pltpu.VMEM((2, LANES, TILE), BF16),
        pltpu.SMEM((TAPS,), F32),
        dma((3,)),
        dma((12,)),
        dma((2, 12)),
        dma((2,)),
        dma((2,)),
        dma((4,)),
    ]
    model, dual, misfits = pl.pallas_call(
        kernel,
        out_shape=(
            pltpu.VMEM((4, 64, 512), F32),
            pltpu.VMEM((3, 4, 64, 512), F32),
            pltpu.VMEM((1, LANES), F32),
        ),
        in_specs=[
            pl.BlockSpec(memory_space=pl.ANY),
            pl.BlockSpec(memory_space=pl.ANY),
            pl.BlockSpec(memory_space=pl.ANY),
        ],
        out_specs=(
            pl.BlockSpec(memory_space=pltpu.VMEM),
            pl.BlockSpec(memory_space=pltpu.VMEM),
            pl.BlockSpec(memory_space=pltpu.VMEM),
        ),
        scratch_shapes=scratch,
        compiler_params=pltpu.CompilerParams(
            collective_id=0, has_side_effects=True, vmem_limit_bytes=40 * 1024 * 1024
        ),
    )(*[pltpu.with_memory_space_constraint(x, pltpu.HBM) for x in (observed, start_model, wavelet)])
    return pl.pallas_call(
        write_out,
        out_shape=(
            jax.ShapeDtypeStruct((4, 64, 512), F32),
            jax.ShapeDtypeStruct((3, 4, 64, 512), F32),
            jax.ShapeDtypeStruct((ITERS,), F32),
        ),
        in_specs=[pl.BlockSpec(memory_space=pltpu.VMEM)] * 3,
        out_specs=(pl.BlockSpec(memory_space=pl.ANY),) * 3,
        scratch_shapes=[pltpu.SMEM((ITERS,), F32), pltpu.SemaphoreType.DMA((3,))],
    )(*[pltpu.with_memory_space_constraint(x, pltpu.VMEM) for x in (model, dual, misfits)])


def solution(mesh):
    sizes = dict(mesh.shape)
    body = functools.partial(shards, sizes["inline"], sizes["xline"] * sizes["tm"])
    in_specs = (P("inline", "xline", "tm"), P("inline", "xline", "tm"), P())
    out_specs = (P("inline", "xline", "tm"), P(None, "inline", "xline", "tm"), P())
    return jax.shard_map(body, mesh=mesh, in_specs=in_specs, out_specs=out_specs, check_vma=False)
```

```python
import functools

import jax
import jax.numpy as jnp
from jax import lax
from jax.experimental import pallas as pl
from jax.experimental.pallas import tpu as pltpu
from jax.sharding import PartitionSpec as P

TAPS = 64
ITERS = 4
LANES = 128
TILE = 256
ROWS = 16
MESH = pl.DeviceIdType.MESH
F32 = jnp.float32
BF16 = jnp.bfloat16

tau_step = 0.1
sigma_step = 0.5
tv_weight = 1.0
x_scale = tau_step * sigma_step

TO_HI, TO_LO, TO_JLO, TO_JHI, TO_THI, TO_TLO, E_IMJP, E_IPJM, E_IMTP, E_IPTM, E_JMTP, E_JPTM = range(12)
MESSAGES = {
    TO_HI: (1, 0, 0),
    TO_LO: (-1, 0, 0),
    TO_JLO: (0, -1, 0),
    TO_JHI: (0, 1, 0),
    TO_THI: (0, 0, 1),
    TO_TLO: (0, 0, -1),
    E_IMJP: (1, -1, 0),
    E_IPJM: (-1, 1, 0),
    E_IMTP: (1, 0, -1),
    E_IPTM: (-1, 0, 1),
    E_JMTP: (0, 1, -1),
    E_JPTM: (0, -1, 1),
}

EDGES = (E_IMTP, E_IPTM, E_IMJP, E_IPJM, E_JMTP, E_JPTM)
TIMES = (TO_THI, TO_TLO)
FACES = (TO_HI, TO_LO, TO_JLO, TO_JHI)
GROUP = {**{k: 0 for k in EDGES}, **{k: 1 for k in TIMES}, **{k: 2 + g for g, k in enumerate(FACES)}}


def split(x):
    hi = x.astype(BF16)
    lo = (x - hi.astype(F32)).astype(BF16)
    return hi, lo


def lane_ids(shape):
    return lax.broadcasted_iota(jnp.int32, shape, len(shape) - 1)


def circulant(row):
    sub = lax.broadcasted_iota(jnp.int32, (8, TILE), 0)
    first = row
    for s in range(1, 8):
        first = jnp.where(sub == s, pltpu.roll(row, s, 1), first)
    return jnp.concatenate([first] + [pltpu.roll(first, 8 * g, 1) for g in range(1, TILE // 8)], axis=0)


def dot32(a, b):
    return jnp.dot(a, b, preferred_element_type=F32, precision=lax.Precision.HIGHEST)


def kernel(
    obs_hbm, start_hbm, wav_hbm, mout, dout, misf,
    X, ms, obs, grad, mnew, xnew, mc, ril, rih, rjl, rjh, rt, rol, roh,
    edge_in, edge_out, jlo, jhi, st, olo, ohi,
    pd0, pd1, pd2, pm, pj, part, allsum, r1, r2,
    tG, tA0, tA1, tB, hG, hA, hB,
    wav, in_sem, send_sem, recv_sem, osend, orecv, sum_sem,
):
    n_i, n_j, n_t = lax.axis_size("inline"), lax.axis_size("xline"), lax.axis_size("tm")
    me_i, me_j, me_t = lax.axis_index("inline"), lax.axis_index("xline"), lax.axis_index("tm")

    def at(di, dj, dt):
        return (
            lax.rem(me_i + (di + n_i), n_i),
            lax.rem(me_j + (dj + n_j), n_j),
            lax.rem(me_t + (dt + n_t), n_t),
        )

    i_peers = sorted([(d, 0, 0) for d in range(1, n_i)], key=lambda o: -min(o[0], n_i - o[0]))
    p_peers = sorted(
        [(0, d // n_t, d % n_t) for d in range(1, n_j * n_t)],
        key=lambda o: -(min(o[1], n_j - o[1]) + min(o[2], n_t - o[2])),
    )
    near_by = [tuple(o % n for o, n in zip(off, (n_i, n_j, n_t))) for off in reversed(MESSAGES.values())]
    friends = list(dict.fromkeys(near_by + [(5, 0, 0), (n_i - 5, 0, 0)]))

    barrier = pltpu.get_barrier_semaphore()
    for off in friends:
        pl.semaphore_signal(barrier, inc=1, device_id=at(*off), device_id_type=MESH)

    loads = []
    for b in range(4):
        cols = pl.ds(b * LANES, LANES)
        loads.append(pltpu.make_async_copy(start_hbm.at[:, :, cols], ms.at[:, b], in_sem.at[0]))
    for b in range(4):
        cols = pl.ds(b * LANES, LANES)
        loads.append(pltpu.make_async_copy(obs_hbm.at[:, :, cols], obs.at[:, b], in_sem.at[1]))
    loads.append(pltpu.make_async_copy(wav_hbm, wav, in_sem.at[2]))
    for load in loads:
        load.start()

    def all_of(ref, sem):
        return pltpu.make_async_copy(ref, ref, sem)

    not_i0 = (me_i > 0).astype(F32)
    not_in = (me_i < n_i - 1).astype(F32)
    not_j0 = (me_j > 0).astype(F32)
    not_jn = (me_j < n_j - 1).astype(F32)
    not_t0 = (me_t > 0).astype(F32)
    not_tn = (me_t < n_t - 1).astype(F32)

    def build_tables():
        ids = lane_ids((8, TILE))
        w = jnp.zeros((8, TILE), F32)
        for k in range(TAPS):
            w = jnp.where(ids == k, wav[k], w)
        c = w - pltpu.roll(w, 1, 1)
        half = TAPS // 2 + 1
        circ_g = circulant(pltpu.roll(c, TILE - half, 1))
        rev = jnp.zeros((8, TILE), F32)
        for k in range(TAPS + 1):
            left = wav[k] if k < TAPS else 0.0
            right = wav[k - 1] if k > 0 else 0.0
            rev = jnp.where(ids == (half - k) % TILE, left - right, rev)
        circ_d = circulant(rev)
        r = lax.broadcasted_iota(jnp.int32, (TILE, TILE), 0)
        near = jnp.abs(r - lane_ids((TILE, TILE))) < LANES

        def store(table, rows, value):
            table[0, rows : rows + TILE, :], table[1, rows : rows + TILE, :] = split(value)

        def store_halo(table, far):
            value = jnp.concatenate([far[LANES:TILE, 0:LANES], far[0:LANES, LANES:TILE]], axis=1)
            table[0], table[1] = split(value)

        g_far = jnp.where(near, 0.0, circ_g)
        d_far = jnp.where(near, 0.0, circ_d)
        store(tG, 0, jnp.where(near, circ_g, 0.0))
        store(tG, TILE, g_far)
        store(tB, 0, jnp.where(near, tau_step * circ_d, 0.0))
        store(tB, TILE, tau_step * d_far)
        store_halo(hG, g_far)
        store_halo(hB, tau_step * d_far)
        circ_a = dot32(circ_g, tau_step * circ_d)
        edge = dot32(g_far, tau_step * d_far)
        a_near = jnp.where(near, circ_a, 0.0)
        a_far = jnp.where(near, 0.0, circ_a)
        store(tA0, 0, a_near - jnp.where(r < LANES, (1.0 - not_t0) * edge, 0.0))
        store(tA0, TILE, a_far)
        store(tA1, 0, a_near - jnp.where(r < LANES, 0.0, (1.0 - not_tn) * edge))
        store(tA1, TILE, a_far)
        store_halo(hA, a_far)


    low_lanes = lane_ids((1, 1, LANES)) < LANES // 2
    lane_valid = jnp.where(low_lanes, not_tn, not_t0)
    last_lane = lane_ids((1, 1, LANES)) == LANES - 1
    first_lane = lane_ids((1, 1, LANES)) == 0

    def pack_time(block3, block0, low_ref, high_ref):
        high_ref[...] = jnp.where(low_lanes, pltpu.roll(block3[:, 32:64], 64, 2), block3[:, 0:32])
        low_ref[...] = jnp.where(low_lanes, block0[:, 0:32], pltpu.roll(block0[:, 32:64], 64, 2))

    def unpack_time(from_low, from_high):
        top = jnp.where(low_lanes, from_high, from_low)
        bottom = pltpu.roll(jnp.where(low_lanes, from_low, from_high), 64, 2)
        return jnp.concatenate([top, bottom], axis=1) * lane_valid

    def message(n, k):
        src, dst = {
            TO_HI: lambda: (X.at[n, 3, 0:4, 0:64, :], ril.at[n, 0:4, 0:64, :]),
            TO_LO: lambda: (X.at[n, 0, 0:4, 0:64, :], rih.at[n, 0:4, 0:64, :]),
            TO_JLO: lambda: (jlo.at[n, :, 0:4, :], rjh.at[n, :, 0:4, :]),
            TO_JHI: lambda: (jhi.at[n, :, 0:4, :], rjl.at[n, :, 0:4, :]),
            TO_THI: lambda: (st.at[n, 0], rt.at[n, 0]),
            TO_TLO: lambda: (st.at[n, 1], rt.at[n, 1]),
            E_IMTP: lambda: (edge_out.at[n, 0:8], edge_in.at[n, 0:8]),
            E_IPTM: lambda: (edge_out.at[n, 8:16], edge_in.at[n, 8:16]),
            E_IMJP: lambda: (edge_out.at[n, 16:20], edge_in.at[n, 16:20]),
            E_IPJM: lambda: (edge_out.at[n, 20:24], edge_in.at[n, 20:24]),
            E_JMTP: lambda: (edge_out.at[n, 24:28], edge_in.at[n, 24:28]),
            E_JPTM: lambda: (edge_out.at[n, 28:32], edge_in.at[n, 28:32]),
        }[k]()
        return pltpu.make_async_remote_copy(
            src_ref=src, dst_ref=dst, send_sem=send_sem.at[GROUP[k]], recv_sem=recv_sem.at[n % 2, GROUP[k]],
            device_id=at(*MESSAGES[k]), device_id_type=MESH,
        )

    def o_message(k):
        src, dst, off = ((ohi, rol, (0, 0, 1)), (olo, roh, (0, 0, -1)))[k]
        return pltpu.make_async_remote_copy(
            src_ref=src, dst_ref=dst, send_sem=osend.at[k], recv_sem=orecv.at[k],
            device_id=at(*off), device_id_type=MESH,
        )

    def sum_message(stage, d):
        if stage == 0:
            src, dst, off = part, r1.at[d], i_peers[d]
        else:
            src, dst, off = allsum, r2.at[d], p_peers[d]
        return pltpu.make_async_remote_copy(
            src_ref=src, dst_ref=dst, send_sem=sum_sem.at[2 * stage], recv_sem=sum_sem.at[2 * stage + 1],
            device_id=at(*off), device_id_type=MESH,
        )

    def pack(n):
        for i in range(4):
            jlo[n, :, i : i + 1, :] = X[n, i, 0:4, 0:1, :]
            jhi[n, :, i : i + 1, :] = X[n, i, 0:4, 63:64, :]
        ids = lane_ids((8, LANES))
        low = X[n, 3, 0, 0:8, :]
        high = pltpu.roll(X[n, 0, 3, 0:8, :], 1, 1)
        for k in range(1, 8):
            low = jnp.where(ids == k, pltpu.roll(X[n, 3, 0, 8 * k : 8 * k + 8, :], k, 1), low)
            high = jnp.where(ids == k, pltpu.roll(X[n, 0, 3, 8 * k : 8 * k + 8, :], k + 1, 1), high)
        edge_out[n, 0:8, :] = low
        edge_out[n, 8:16, :] = high
        for b in range(4):
            edge_out[n, 16 + b : 17 + b, :] = X[n, 3, b, 0:1, :]
            edge_out[n, 20 + b : 21 + b, :] = X[n, 0, b, 63:64, :]
            edge_out[n, 24 + b : 25 + b, :] = X[n, b, 0, 63:64, :]
            edge_out[n, 28 + b : 29 + b, :] = X[n, b, 3, 0:1, :]

    def sent(n, kinds):
        if kinds == EDGES:
            all_of(edge_out.at[n], send_sem.at[0]).wait()
        elif kinds == TIMES:
            all_of(st.at[n], send_sem.at[1]).wait()
        else:
            for k in kinds:
                message(n, k).wait_send()

    def start(n, *groups):
        for kinds in groups:
            if n > 0:
                sent(n - 1, kinds)
            for k in kinds:
                message(n, k).start()

    def send_time(n):
        pack_time(ms[:, 3], ms[:, 0], st.at[n, 1], st.at[n, 0])
        start(n, TIMES)

    def send(n):
        pack(n)
        if n < ITERS - 1:
            start(n, EDGES, FACES[0:2], TIMES, FACES[2:4])
        else:
            start(n, EDGES, FACES)

    def receive_time(n):
        all_of(rt.at[n], recv_sem.at[n % 2, 1]).wait()
        halo = unpack_time(rt[n, 0], rt[n, 1])
        if n == 0:
            X[n, :, 4, 0:64, :] = x_scale * halo
        else:
            X[n, :, 4, 0:64, :] = 2.0 * x_scale * halo - x_scale * mc[...]
        mc[...] = halo

    def receive_rest(n):
        all_of(edge_in.at[n], recv_sem.at[n % 2, 0]).wait()
        for k in FACES:
            message(n, k).wait_recv()
        for i in range(4):
            X[n, i, 0:4, 64:65, :] = rjh[n, :, i : i + 1, :] * not_jn
            X[n, i, 4, 64:65, :] = edge_in[n, 28 + i : 29 + i, :] * not_jn
        for b in range(4):
            ril[n, b, 64:65, :] = edge_in[n, 16 + b : 17 + b, :] * not_jn
        low = edge_in[n, 0:8, :] * not_tn
        high = edge_in[n, 8:16, :] * not_t0
        for k in range(8):
            rows = slice(8 * k, 8 * k + 8)
            ril[n, 4, rows, :] = low if k == 0 else pltpu.roll(low, LANES - k, 1)
            rih[n, 4, rows, :] = pltpu.roll(high, LANES - 1 - k, 1)

    def flat(block):
        return split(block.reshape(4 * 64, LANES))

    def join(pieces):
        return tuple(jnp.concatenate([p[k] for p in pieces], axis=1) for k in range(2))

    def product(x, table, start, stop):
        hi, lo = x
        dot = lambda a, b: jnp.dot(a, b, preferred_element_type=F32)
        return dot(hi, table[0, start:stop]) + dot(lo, table[0, start:stop]) + dot(hi, table[1, start:stop])

    def own_part(m, first, second):
        return [
            product(join([m[0], m[1], m[2]]), first, 0, 3 * LANES),
            product(join([m[2], m[3]]), second, 0, 2 * LANES) + product(m[1], second, 3 * LANES, 4 * LANES),
        ]

    def halo_part(c, table):
        return product(c, table, 0, LANES)

    def put(ref, values):
        for half, value in enumerate(values):
            for b in range(2):
                ref[:, 2 * half + b] = value[:, b * LANES : (b + 1) * LANES].reshape(4, 64, LANES)

    def prepare(values):
        for half, value in enumerate(values):
            for b in range(2):
                k = 2 * half + b
                model = ms[:, k]
                new = model - (value[:, b * LANES : (b + 1) * LANES].reshape(4, 64, LANES) - grad[:, k])
                mnew[:, k] = new
                xnew[:, k] = (2.0 * x_scale) * new - x_scale * model

    def add_halo(value, sign):
        for k, b in enumerate((0, 3)):
            term = sign * value[:, k * LANES : (k + 1) * LANES].reshape(4, 64, LANES)
            mnew[:, b] = mnew[:, b] + term
            xnew[:, b] = xnew[:, b] + (2.0 * x_scale) * term

    def squares(e):
        return jnp.sum((e * e).reshape(4 * 8, 8, LANES), axis=0)

    def own_residual(m):
        left, right = own_part(m, tG, tG)
        blocks = [left[:, 0:LANES], left[:, LANES:TILE], right[:, 0:LANES], right[:, LANES:TILE]]
        e = [block - obs[:, b].reshape(4 * 64, LANES) for b, block in enumerate(blocks)]
        return e[0], e[3], squares(e[1]) + squares(e[2])

    def sum_up(n, own, c):
        first, last, total = own
        h = halo_part(c, hG)
        total = total + squares(first + h[:, 0:LANES]) + squares(last + h[:, LANES:TILE])
        line = jnp.sum(jnp.sum(total, axis=0, keepdims=True), axis=1, keepdims=True)
        lane = lane_ids((1, LANES))
        part[...] = jnp.where(lane == n, line, 0.0 if n == 0 else part[...])

    def shrink(q0, q1, q2):
        scale = jnp.minimum(1.0, tau_step * tv_weight * lax.rsqrt(q0 * q0 + q1 * q1 + q2 * q2))
        return q0 * scale, q1 * scale, q2 * scale

    def next_sample(x):
        moved = pltpu.roll(x, LANES - 1, 2)
        ahead = jnp.concatenate([moved[1:], moved[:1]], axis=0)
        return jnp.where(last_lane, ahead, moved)

    def trial(old, new, x):
        return new - x if old is None else old + (new - x)

    def dual_below(n):
        def chunk(k, carry):
            rows = pl.ds(k * ROWS, ROWS)
            x5 = ril[n, :, rows, :]
            x = x5[0:4]
            xt = next_sample(x5)[0:4]
            xj = ril[n, 0:4, pl.ds(k * ROWS + 1, ROWS), :]
            xi = X[n, 0, 0:4, rows, :]
            old = [None] * 3 if n == 0 else [pm[c, :, rows, :] for c in range(3)]
            p0, p1, p2 = shrink(trial(old[0], xi, x), trial(old[1], xj, x), trial(old[2], xt, x))
            pm[0, :, rows, :] = p0 * not_i0
            pm[1, :, rows, :] = p1
            pm[2, :, rows, :] = p2
            return carry

        lax.fori_loop(0, 64 // ROWS, chunk, 0, unroll=True)

    def dual_before(n):
        row = lax.broadcasted_iota(jnp.int32, (1, 8, LANES), 1)
        above = jnp.concatenate([jnp.broadcast_to(edge_in[n, 20 + b : 21 + b, :], (8, LANES))[None] for b in range(4)], axis=0)
        above = above * not_in
        x = jnp.where(row < 4, rjl[n], above)
        x5 = jnp.concatenate([x, (edge_in[n, 24:32, :] * not_tn)[None]], axis=0)
        xt = next_sample(x5)[0:4]
        xi = pltpu.roll(x, 7, 1)
        xj = jlo[n]
        old = [None] * 3 if n == 0 else [pj[c] for c in range(3)]
        p0, p1, p2 = shrink(trial(old[0], xi, x), trial(old[1], xj, x), trial(old[2], xt, x))
        pj[0] = p0
        pj[1] = p1
        pj[2] = p2
        p1 = p1 * not_j0
        for i in range(4):
            pd1[i, 0:4, 7:8, :] = p1[:, i : i + 1, :]

    def dual_part(n, i, start, count, blocks):
        rows, shifted = pl.ds(start, count), pl.ds(start + 8, count)
        lo, hi = blocks
        cut = slice(lo, hi)
        x = X[n, i, cut, rows, :]
        after = X[n, i, hi % 5, rows, :][None]
        moved = pltpu.roll(x, LANES - 1, 2)
        ahead = jnp.concatenate([moved[1:], pltpu.roll(after, LANES - 1, 2)], axis=0)
        xt = jnp.where(last_lane, ahead, moved)
        xj = X[n, i, cut, pl.ds(start + 1, count), :]
        xi = X[n, i + 1, cut, rows, :] if i < 3 else rih[n, cut, rows, :] * not_in
        if n == 0:
            old = [None] * 3
        else:
            old = [pd0[i, cut, rows, :], pd1[i, cut, shifted, :], pd2[i, cut, rows, :]]
        p0, p1, p2 = shrink(trial(old[0], xi, x), trial(old[1], xj, x), trial(old[2], xt, x))
        pd0[i, cut, rows, :] = p0
        pd1[i, cut, shifted, :] = p1
        pd2[i, cut, rows, :] = p2
        if n == ITERS - 1:
            for b in range(lo, min(hi, 4)):
                cols = pl.ds(b * LANES, LANES)
                dout[0, i, rows, cols] = p0[b - lo] * (1.0 / tau_step)
                dout[1, i, rows, cols] = p1[b - lo] * (1.0 / tau_step)
                dout[2, i, rows, cols] = p2[b - lo] * (1.0 / tau_step)

    def dual_inside(n):
        for i in range(3):
            for start, count in ((0, 16), (16, 16), (32, 16), (48, 8)):
                dual_part(n, i, start, count, (0, 3))

    def dual_outside(n):
        dual_below(n)
        dual_before(n)
        for i in range(3):
            for start, count in ((0, 16), (16, 16), (32, 16), (48, 8)):
                dual_part(n, i, start, count, (3, 5))
            dual_part(n, i, 56, 8, (0, 5))
        for start in range(0, 64, 16):
            dual_part(n, 3, start, 16, (0, 5))

    def update(n, i, blocks):
        last = n == ITERS - 1
        lo, hi = blocks

        def chunk(k, carry):
            rows = pl.ds(k * ROWS, ROWS)
            cut = slice(lo, hi)
            p2 = pd2[i, cut, rows, :]
            ahead = pd2[i, (lo - 1) % 5, rows, :][None]
            if lo == 0:
                ahead = ahead * not_t0
            moved = pltpu.roll(p2, 1, 2)
            behind = pltpu.roll(ahead, 1, 2)
            if hi - lo > 1:
                behind = jnp.concatenate([behind, moved[:-1]], axis=0)
            before0 = pm[0, cut, rows, :] if i == 0 else pd0[i - 1, cut, rows, :]
            before1 = pd1[i, cut, pl.ds(k * ROWS + 7, ROWS), :]
            tv_term = before0 - pd0[i, cut, rows, :]
            tv_term = tv_term + (before1 - pd1[i, cut, pl.ds(k * ROWS + 8, ROWS), :])
            tv_term = tv_term + (jnp.where(first_lane, behind, moved) - p2)
            updated = mnew[i, cut, rows, :] - tv_term
            if last:
                for b in range(lo, hi):
                    mout[i, rows, pl.ds(b * LANES, LANES)] = updated[b - lo]
            else:
                ms[i, cut, rows, :] = updated
                X[n + 1, i, cut, rows, :] = xnew[i, cut, rows, :] - (2.0 * x_scale) * tv_term
            return carry

        lax.fori_loop(0, 64 // ROWS, chunk, 0, unroll=True)

    all_of(ms, in_sem.at[0]).wait()
    X[0, :, 0:4, 0:64, :] = x_scale * ms[...]
    pack_time(ms[:, 3], ms[:, 0], st.at[0, 1], st.at[0, 0])
    pl.semaphore_wait(barrier, len(friends))
    send(0)
    all_of(obs, in_sem.at[1]).wait()
    loads[8].wait()
    pack_time(obs[:, 3], obs[:, 0], olo, ohi)
    o_message(0).start()
    o_message(1).start()
    build_tables()
    put(grad, own_part([flat(obs[:, b]) for b in range(4)], tB, tB))

    kept = None
    for n in range(ITERS):
        if n > 0:
            sum_up(n - 1, own_residual(kept[0]), kept[1])
        own = [flat(ms[:, b]) for b in range(4)]
        prepare(own_part(own, tA0, tA1))
        dual_inside(n)
        if n == ITERS - 1:
            last = own_residual(own)
            receive_time(n)
            halo = flat(mc[...])
            sum_up(n, last, halo)
            for d in range(len(i_peers)):
                sum_message(0, d).start()
            receive_rest(n)
        else:
            receive_time(n)
            receive_rest(n)
            halo = flat(mc[...])
            kept = (own, halo)
        add_halo(halo_part(halo, hA), -1.0)
        dual_outside(n)
        if n == 0:
            o_message(0).wait_recv()
            o_message(1).wait_recv()
            value = halo_part(flat(unpack_time(rol[...], roh[...])), hB)
            add_halo(value, 1.0)
            for k, b in enumerate((0, 3)):
                grad[:, b] = grad[:, b] + value[:, k * LANES : (k + 1) * LANES].reshape(4, 64, LANES)
        if n == ITERS - 2:
            for i in range(4):
                update(n, i, (0, 1))
                update(n, i, (3, 4))
            send_time(n + 1)
            for i in range(4):
                update(n, i, (1, 3))
            send(n + 1)
        else:
            for i in range(4):
                update(n, i, (0, 4))
            if n < ITERS - 1:
                pack_time(ms[:, 3], ms[:, 0], st.at[n + 1, 1], st.at[n + 1, 0])
                send(n + 1)

    total = part[...]
    all_of(r1, sum_sem.at[1]).wait()
    for d in range(len(i_peers)):
        total = total + r1[d]
    allsum[...] = total
    for d in range(len(p_peers)):
        sum_message(1, d).start()

    total = allsum[...]
    all_of(r2, sum_sem.at[3]).wait()
    for d in range(len(p_peers)):
        total = total + r2[d]
    cells = 4 * 64 * 512 * n_i * n_j * n_t
    misf[...] = total * (1.0 / cells)

    for kinds in (EDGES, TIMES, FACES):
        sent(ITERS - 1, kinds)
    o_message(0).wait_send()
    o_message(1).wait_send()
    all_of(r1, sum_sem.at[0]).wait()
    all_of(r2, sum_sem.at[2]).wait()


def write_out(model, dual, misfits, model_out, dual_out, misfits_out, line, sem):
    pairs = ((dual, dual_out), (model, model_out), (line, misfits_out))
    copies = [pltpu.make_async_copy(src, dst, sem.at[k]) for k, (src, dst) in enumerate(pairs)]
    copies[0].start()
    copies[1].start()
    for n in range(ITERS):
        line[n] = misfits[0, n]
    copies[2].start()
    for copy in copies:
        copy.wait()


def shards(n_inline, n_plane, observed, start_model, wavelet):
    dma = pltpu.SemaphoreType.DMA
    v = lambda *shape: pltpu.VMEM(shape, F32)
    scratch = [
        v(ITERS, 4, 5, 72, LANES),
        v(4, 4, 64, LANES),
        v(4, 4, 64, LANES),
        v(4, 4, 64, LANES),
        v(4, 4, 64, LANES),
        v(4, 4, 64, LANES),
        v(4, 64, LANES),
        v(ITERS, 5, 72, LANES),
        v(ITERS, 5, 64, LANES),
        v(ITERS, 4, 8, LANES),
        v(ITERS, 4, 8, LANES),
        v(ITERS, 2, 4, 32, LANES),
        v(4, 32, LANES),
        v(4, 32, LANES),
        v(ITERS, 32, LANES),
        v(ITERS, 32, LANES),
        v(ITERS, 4, 8, LANES),
        v(ITERS, 4, 8, LANES),
        v(ITERS, 2, 4, 32, LANES),
        v(4, 32, LANES),
        v(4, 32, LANES),
        v(4, 5, 64, LANES),
        v(4, 5, 72, LANES),
        v(4, 5, 64, LANES),
        v(3, 4, 64, LANES),
        v(3, 4, 8, LANES),
        v(1, LANES),
        v(1, LANES),
        v(n_inline - 1, 1, LANES),
        v(n_plane - 1, 1, LANES),
        pltpu.VMEM((2, 2 * TILE, TILE), BF16),
        pltpu.VMEM((2, 2 * TILE, TILE), BF16),
        pltpu.VMEM((2, 2 * TILE, TILE), BF16),
        pltpu.VMEM((2, 2 * TILE, TILE), BF16),
        pltpu.VMEM((2, LANES, TILE), BF16),
        pltpu.VMEM((2, LANES, TILE), BF16),
        pltpu.VMEM((2, LANES, TILE), BF16),
        pltpu.SMEM((TAPS,), F32),
        dma((3,)),
        dma((6,)),
        dma((2, 6)),
        dma((2,)),
        dma((2,)),
        dma((4,)),
    ]
    model, dual, misfits = pl.pallas_call(
        kernel,
        out_shape=(
            pltpu.VMEM((4, 64, 512), F32),
            pltpu.VMEM((3, 4, 64, 512), F32),
            pltpu.VMEM((1, LANES), F32),
        ),
        in_specs=[
            pl.BlockSpec(memory_space=pl.ANY),
            pl.BlockSpec(memory_space=pl.ANY),
            pl.BlockSpec(memory_space=pl.ANY),
        ],
        out_specs=(
            pl.BlockSpec(memory_space=pltpu.VMEM),
            pl.BlockSpec(memory_space=pltpu.VMEM),
            pl.BlockSpec(memory_space=pltpu.VMEM),
        ),
        scratch_shapes=scratch,
        compiler_params=pltpu.CompilerParams(
            collective_id=0, has_side_effects=True, vmem_limit_bytes=40 * 1024 * 1024
        ),
    )(*[pltpu.with_memory_space_constraint(x, pltpu.HBM) for x in (observed, start_model, wavelet)])
    return pl.pallas_call(
        write_out,
        out_shape=(
            jax.ShapeDtypeStruct((4, 64, 512), F32),
            jax.ShapeDtypeStruct((3, 4, 64, 512), F32),
            jax.ShapeDtypeStruct((ITERS,), F32),
        ),
        in_specs=[pl.BlockSpec(memory_space=pltpu.VMEM)] * 3,
        out_specs=(pl.BlockSpec(memory_space=pl.ANY),) * 3,
        scratch_shapes=[pltpu.SMEM((ITERS,), F32), pltpu.SemaphoreType.DMA((3,))],
    )(*[pltpu.with_memory_space_constraint(x, pltpu.VMEM) for x in (model, dual, misfits)])


def solution(mesh):
    sizes = dict(mesh.shape)
    body = functools.partial(shards, sizes["inline"], sizes["xline"] * sizes["tm"])
    in_specs = (P("inline", "xline", "tm"), P("inline", "xline", "tm"), P())
    out_specs = (P("inline", "xline", "tm"), P(None, "inline", "xline", "tm"), P())
    return jax.shard_map(body, mesh=mesh, in_specs=in_specs, out_specs=out_specs, check_vma=False)
```
